32 devices in a mesh: fsdp: 4 (over y, x), ctx: 8 (over z, core).
Axes of the slice: x: 2, y: 2, z: 4, core: 2. Of those that a mesh axis runs over, the one named last changes fastest.
Arguments:
- tokens: bfloat16 [8192, 768], P(('fsdp', 'ctx')), may hold values from -6 to 6
- cotangent: bfloat16 [8192, 768], P(('fsdp', 'ctx')), may hold values from -6 to 6
- lengths: int32 [4], P('fsdp'), may hold values from 256 to 2048, as said below
- block_table: int32 [16], replicated, may hold values from 0 to 15, each once
- qkv_weight: bfloat16 [768, 2304], P('fsdp'), may hold values from -0.21875 to 0.21875
- query_bias: bfloat16 [768], P('fsdp'), may hold values from -3 to 3
- value_bias: bfloat16 [768], P('fsdp'), may hold values from -0.039794922 to 0.039794922
- proj_weight: bfloat16 [768, 768], P('fsdp')
- proj_bias: bfloat16 [768], P('fsdp'), may hold values from -3 to 3
- gain_first: bfloat16 [768], P('fsdp'), may hold values from 0.5 to 1.5
- shift_first: bfloat16 [768], P('fsdp'), may hold values from -3 to 3
- inner_weight: bfloat16 [768, 3072], P('fsdp'), may hold values from -0.21875 to 0.21875
- inner_bias: bfloat16 [3072], P('fsdp'), may hold values from -3 to 3
- outer_weight: bfloat16 [3072, 768], P('fsdp'), may hold values from -0.109375 to 0.109375
- outer_bias: bfloat16 [768], P('fsdp'), may hold values from -3 to 3
- gain_second: bfloat16 [768], P('fsdp'), may hold values from 0.5 to 1.5
- shift_second: bfloat16 [768], P('fsdp'), may hold values from -3 to 3
Outputs:
- layer_out: bfloat16 [8192, 768], P(('fsdp', 'ctx'))
- tokens_grad: bfloat16 [8192, 768], P(('fsdp', 'ctx'))
- qkv_weight_grad: float32 [768, 2304], P('fsdp')
- query_bias_grad: float32 [768], P('fsdp')
- value_bias_grad: float32 [768], P('fsdp')
- proj_weight_grad: float32 [768, 768], P('fsdp')
- proj_bias_grad: float32 [768], P('fsdp')
- gain_first_grad: float32 [768], P('fsdp')
- shift_first_grad: float32 [768], P('fsdp')
- inner_weight_grad: float32 [768, 3072], P('fsdp')
- inner_bias_grad: float32 [3072], P('fsdp')
- outer_weight_grad: float32 [3072, 768], P('fsdp')
- outer_bias_grad: float32 [768], P('fsdp')
- gain_second_grad: float32 [768], P('fsdp')
- shift_second_grad: float32 [768], P('fsdp')
The draws below stay inside these ranges and needn't reach their ends.
Inputs may be any that keep to these rules, and one draw needn't show every extreme that they name: `lengths`: one sequence is full. `block_table`: each value appears once.
All inputs are finite; a program needn't handle non-finite values.
Results may differ from the reference program's by a relative error of at most 0.02.
Values may be sent and summed in bfloat16 or wider, within the bound.
A program may use at most 320 MiB of HBM per device.

```python
import math
import jax
import jax.numpy as jnp
from jax import lax

D = 768
HEADS = 12
HEAD_DIM = 64
FF = 3072
BLK = 128
NBLK = 16
LEN = 2048
SEQS = 4
TOKENS = 8192


def draw_lengths(key, part):
    first_key, second_key = jax.random.split(jax.random.fold_in(key, 11))
    drawn = jax.random.randint(first_key, (SEQS,), LEN // 8, LEN + 1, dtype=jnp.int32)
    chosen = jax.random.randint(second_key, (), 0, SEQS, dtype=jnp.int32)
    return jnp.where(jnp.arange(SEQS, dtype=jnp.int32) == chosen, LEN, drawn).astype(jnp.int32)


def draw_proj_weight(key, part):
    normal_draw = jax.random.normal(jax.random.fold_in(key, 23), (D, D), jnp.float32)
    return (normal_draw * jnp.sqrt(LEN / (4.0 * D))).astype(jnp.bfloat16)


def shard_levels(stream_key, dims, cuts, least, high):
    def one(position, blocks):
        heights = jax.random.uniform(jax.random.fold_in(jax.random.fold_in(stream_key, 6), position), (blocks,), jnp.float32, least / len(cuts), high / len(cuts))
        return jnp.repeat(jnp.exp(heights), dims[position] // blocks).reshape((-1,) + (1,) * (len(dims) - position - 1))

    level = one(*cuts[0])
    for cut in cuts[1:]:
        level = level * one(*cut)
    return level


def bell_draw(key, dims, deviation, reach, cuts=(), held_as=jnp.bfloat16):
    loudness = shard_levels(key, dims, cuts, -0.22, 0.18) if cuts else 1.0
    values = jax.random.normal(key, dims, jnp.float32) * deviation * loudness
    return jnp.minimum(jnp.maximum(values, -reach), reach).astype(held_as)


def setup_inputs(seed: int = 0) -> dict:
    keys = jax.random.split(jax.random.key(seed), 18)
    tokens = bell_draw(keys[0], (TOKENS, D), 1.0, 6.0, ((0, 32),))
    cotangent = bell_draw(keys[1], (TOKENS, D), 1.0, 6.0, ((0, 32),))
    lengths = draw_lengths(jax.random.fold_in(keys[17], 71), 0)
    block_table = jax.random.permutation(keys[3], NBLK).astype(jnp.int32)
    qkv_weight = bell_draw(keys[4], (D, 3 * D), D ** -0.5, 0.21875, ((0, 4),))
    query_bias = bell_draw(keys[5], (D,), 0.5, 3.0, ((0, 4),))
    value_bias = jnp.clip(jax.random.uniform(keys[6], (D,), jnp.float32, -0.039794922, 0.039794922) * shard_levels(keys[6], (D,), ((0, 4),), -0.4, 0.0), -0.039794922, 0.039794922).astype(jnp.bfloat16)
    proj_weight = draw_proj_weight(jax.random.fold_in(keys[17], 71), 0)
    proj_bias = bell_draw(keys[8], (D,), 0.5, 3.0, ((0, 4),))
    gain_first = jnp.clip(1.0 + 0.1 * jax.random.normal(keys[9], (D,), jnp.float32), 0.5, 1.5).astype(jnp.bfloat16)
    shift_first = bell_draw(keys[10], (D,), 0.5, 3.0, ((0, 4),))
    inner_weight = bell_draw(keys[11], (D, FF), D ** -0.5, 0.21875, ((0, 4),))
    inner_bias = bell_draw(keys[12], (FF,), 0.5, 3.0, ((0, 4),))
    outer_weight = bell_draw(keys[13], (FF, D), FF ** -0.5, 0.109375, ((0, 4),))
    outer_bias = bell_draw(keys[14], (D,), 0.5, 3.0, ((0, 4),))
    gain_second = jnp.clip(1.0 + 0.1 * jax.random.normal(keys[15], (D,), jnp.float32), 0.5, 1.5).astype(jnp.bfloat16)
    shift_second = bell_draw(keys[16], (D,), 0.5, 3.0, ((0, 4),))
    return dict(tokens=tokens, cotangent=cotangent, lengths=lengths, block_table=block_table, qkv_weight=qkv_weight, query_bias=query_bias, value_bias=value_bias, proj_weight=proj_weight, proj_bias=proj_bias, gain_first=gain_first, shift_first=shift_first, inner_weight=inner_weight, inner_bias=inner_bias, outer_weight=outer_weight, outer_bias=outer_bias, gain_second=gain_second, shift_second=shift_second)


NEG_FILL = -1e+30
NORM_EPS = 1e-05

@jax.custom_vjp
def low(v):
    return lax.optimization_barrier(v.astype(jnp.bfloat16)).astype(jnp.float32)

@jax.custom_vjp
def low_back(v):
    return v

def low_keep(v):
    return (low(v), None)

def low_pass(kept, grad):
    return (grad,)

def back_keep(v):
    return (v, None)

def back_low(kept, grad):
    return (low(grad),)
low.defvjp(low_keep, low_pass)
low_back.defvjp(back_keep, back_low)

def matmul_high(first_op, second_op):
    return jnp.dot(first_op, second_op, precision=lax.Precision.HIGHEST, preferred_element_type=jnp.float32)

def layer_norm(vector_in, gain_in, shift_in):
    center = vector_in - lax.optimization_barrier(jnp.mean(vector_in, axis=-1, keepdims=True))
    spread = lax.optimization_barrier(jnp.mean(center * center, axis=-1, keepdims=True))
    return center * lax.rsqrt(spread + NORM_EPS) * gain_in + shift_in

def forward(key_valid_mask, tokens, qkv_weight, query_bias, value_bias, proj_weight, proj_bias, gain_first, shift_first, inner_weight, inner_bias, outer_weight, outer_bias, gain_second, shift_second):
    feat_width = HEADS * HEAD_DIM
    score_scale = 1.0 / math.sqrt(HEAD_DIM)
    bias_row = jnp.concatenate([query_bias, jnp.zeros_like(query_bias), value_bias])
    packed = low(low_back(matmul_high(tokens, qkv_weight) + bias_row))
    packed = packed.reshape(SEQS, LEN, 3 * feat_width)
    blk_size = math.gcd(LEN, 512)

    def one_sequence(loop_item):
        seq_packed, seq_valid = loop_item
        queries = seq_packed[:, :feat_width].reshape(LEN // blk_size, blk_size, HEADS, HEAD_DIM)
        key_rows = seq_packed[:, feat_width:2 * feat_width].reshape(LEN, HEADS, HEAD_DIM)
        value_rows = seq_packed[:, 2 * feat_width:].reshape(LEN, HEADS, HEAD_DIM)

        def one_block(query_blk):
            scores = jnp.einsum('qhd,khd->hqk', query_blk, key_rows, precision=lax.Precision.HIGHEST) * score_scale
            scores = low_back(jnp.where(seq_valid[None, None, :], scores, NEG_FILL))
            attn_probs = low(jax.nn.softmax(scores, axis=-1))
            return jnp.einsum('hqk,khd->qhd', attn_probs, value_rows, precision=lax.Precision.HIGHEST)
        outputs = lax.map(jax.checkpoint(one_block), queries)
        return outputs.reshape(LEN, feat_width)
    attn_vec = lax.map(one_sequence, (packed, key_valid_mask)).reshape(SEQS * LEN, feat_width)
    context = low(low_back(attn_vec))
    proj_out = low_back(matmul_high(context, proj_weight) + proj_bias)
    hidden = tokens + proj_out
    normed = layer_norm(hidden, gain_first, shift_first)
    inner_pre = low_back(matmul_high(low(normed), inner_weight) + inner_bias)
    active = low(jax.nn.gelu(inner_pre, approximate=False))
    branch = low_back(matmul_high(active, outer_weight) + outer_bias)
    return layer_norm(normed + branch, gain_second, shift_second)

def reference(tokens, cotangent, lengths, block_table, qkv_weight, query_bias, value_bias, proj_weight, proj_bias, gain_first, shift_first, inner_weight, inner_bias, outer_weight, outer_bias, gain_second, shift_second):
    stored = jnp.arange(LEN, dtype=jnp.int32)
    placed = block_table[stored // BLK] * BLK + stored % BLK
    key_valid_mask = placed[None, :] < lengths[:, None]
    floats = tuple((param.astype(jnp.float32) for param in (tokens, qkv_weight, query_bias, value_bias, proj_weight, proj_bias, gain_first, shift_first, inner_weight, inner_bias, outer_weight, outer_bias, gain_second, shift_second)))

    def bound_forward(*params):
        return forward(key_valid_mask, *params)
    result, pull_back = jax.vjp(bound_forward, *floats)
    all_grads = pull_back(cotangent.astype(jnp.float32))
    return (result.astype(jnp.bfloat16), all_grads[0].astype(jnp.bfloat16), all_grads[1], all_grads[2], all_grads[3], all_grads[4], all_grads[5], all_grads[6], all_grads[7], all_grads[8], all_grads[9], all_grads[10], all_grads[11], all_grads[12], all_grads[13])
```

```python
import functools
import math

import jax
import jax.numpy as jnp
from jax import lax
from jax.experimental import pallas as pl
from jax.experimental.pallas import tpu as pltpu
from jax.sharding import PartitionSpec as P

HEADS = 12
HEAD_DIM = 64
BLK = 128


NEG_FILL = -1e30
NORM_EPS = 1e-05


def layer_norm(vector_in, gain_in, shift_in):
    center = vector_in - jnp.mean(vector_in, axis=-1, keepdims=True)
    spread = jnp.mean(center * center, axis=-1, keepdims=True)
    return center * lax.rsqrt(spread + NORM_EPS) * gain_in + shift_in


def gelu_exact(vector_in):
    return jax.nn.gelu(vector_in, approximate=False)


def cross_dot(first_op, second_op):
    return lax.dot_general(
        first_op, second_op, (((0,), (0,)), ((), ())), preferred_element_type=jnp.float32
    )


def back_dot(first_op, second_op):
    return lax.dot_general(
        first_op, second_op, (((1,), (1,)), ((), ())), preferred_element_type=jnp.float32
    )


def key_valid(start_row, piece_rows, blk_rows, block_table, seq_length):
    index_rows = start_row + jnp.arange(piece_rows, dtype=jnp.int32)
    owner_block = index_rows // blk_rows
    table_slots = jnp.arange(block_table.shape[0], dtype=jnp.int32)
    placed = jnp.sum(
        jnp.where(owner_block[:, None] == table_slots[None, :], block_table[None, :], 0), axis=1
    )
    return placed * blk_rows + index_rows % blk_rows < seq_length


def exp_scores(query_blk, key_blk, valid_keys, lse_blk, score_scale):
    scores = (
        jnp.einsum("qhd,khd->hqk", query_blk, key_blk, preferred_element_type=jnp.float32)
        * score_scale
    )
    scores = jnp.where(valid_keys[None, None, :], scores, NEG_FILL)
    return jnp.exp(scores - lse_blk[:, :, None])


def exchange_kernel(n, axis, x_ref, y_ref, send_sem, recv_sem, own_sem):
    me = lax.axis_index(axis)
    barrier = pltpu.get_barrier_semaphore()
    for step in range(1, n):
        pl.semaphore_signal(
            barrier,
            inc=1,
            device_id={axis: lax.rem(me + step, n)},
            device_id_type=pl.DeviceIdType.MESH,
        )
    own = pltpu.make_async_copy(x_ref.at[me], y_ref.at[me], own_sem)
    own.start()
    pl.semaphore_wait(barrier, n - 1)
    for step in range(1, n):
        peer = lax.rem(me + step, n)
        pltpu.make_async_remote_copy(
            src_ref=x_ref.at[peer],
            dst_ref=y_ref.at[me],
            send_sem=send_sem.at[step],
            recv_sem=recv_sem.at[step],
            device_id={axis: peer},
            device_id_type=pl.DeviceIdType.MESH,
        ).start()
    own.wait()
    for step in range(1, n):
        source = lax.rem(me + n - step, n)
        copy = pltpu.make_async_remote_copy(
            src_ref=x_ref.at[source],
            dst_ref=y_ref.at[source],
            send_sem=send_sem.at[step],
            recv_sem=recv_sem.at[step],
            device_id={axis: source},
            device_id_type=pl.DeviceIdType.MESH,
        )
        copy.wait()


def exchange(blocks, axis, number):
    n = blocks.shape[0]
    size = 2 * blocks.size * blocks.dtype.itemsize
    return pl.pallas_call(
        functools.partial(exchange_kernel, n, axis),
        out_shape=jax.ShapeDtypeStruct(blocks.shape, blocks.dtype),
        in_specs=[pl.BlockSpec(memory_space=pltpu.VMEM)],
        out_specs=pl.BlockSpec(memory_space=pltpu.VMEM),
        scratch_shapes=[
            pltpu.SemaphoreType.DMA((n,)),
            pltpu.SemaphoreType.DMA((n,)),
            pltpu.SemaphoreType.DMA,
        ],
        compiler_params=pltpu.CompilerParams(
            collective_id=number, has_side_effects=True, vmem_limit_bytes=size + (4 << 20)
        ),
        cost_estimate=pl.CostEstimate(flops=0, bytes_accessed=10 * size, transcendentals=0),
    )(blocks)


QTILE = 512


def attend_kernel(query_ref, key_ref, value_ref, out_ref, lse_ref):
    scores = lax.dot_general(
        key_ref[0], query_ref[...], (((1,), (1,)), ((), ())), preferred_element_type=jnp.float32
    )
    top = jnp.max(scores, axis=0, keepdims=True)
    weights = jnp.exp(scores - top)
    total = jnp.sum(weights, axis=0, keepdims=True)
    out = jnp.dot(value_ref[0], weights.astype(jnp.bfloat16), preferred_element_type=jnp.float32)
    out_ref[...] = out / total
    lse_ref[...] = top + jnp.log(total)


def attend(query, key, value_t):
    rows, keys = query.shape[0], key.shape[1]
    tiles_first = keys // QTILE
    return pl.pallas_call(
        attend_kernel,
        grid=(rows // QTILE,),
        in_specs=[
            pl.BlockSpec((QTILE, 2 * HEAD_DIM), lambda i: (i, 0)),
            pl.BlockSpec((1, keys, 2 * HEAD_DIM), lambda i: (i // tiles_first, 0, 0)),
            pl.BlockSpec((1, HEAD_DIM, keys), lambda i: (i // tiles_first, 0, 0)),
        ],
        out_specs=[
            pl.BlockSpec((HEAD_DIM, QTILE), lambda i: (0, i)),
            pl.BlockSpec((1, QTILE), lambda i: (0, i)),
        ],
        out_shape=[
            jax.ShapeDtypeStruct((HEAD_DIM, rows), jnp.float32),
            jax.ShapeDtypeStruct((1, rows), jnp.float32),
        ],
        compiler_params=pltpu.CompilerParams(vmem_limit_bytes=40 << 20),
        cost_estimate=pl.CostEstimate(
            flops=4 * rows * keys * HEAD_DIM, bytes_accessed=8 << 20, transcendentals=rows * keys
        ),
    )(query, key, value_t)


def attend_back_kernel(
    tiles_first,
    query_ref,
    key_ref,
    key_t_ref,
    value_ref,
    grad_ref,
    out_ref,
    grad_t_ref,
    lse_ref,
    dquery_ref,
    dkey_ref,
    dvalue_ref,
):
    step = pl.program_id(0)
    scores = back_dot(key_ref[0], query_ref[...])
    probs = jnp.exp(scores - lse_ref[...])
    delta = jnp.sum(out_ref[...] * grad_t_ref[...].astype(jnp.float32), axis=0, keepdims=True)
    prob_grad = back_dot(value_ref[0], grad_ref[...])
    score_low = (probs * (prob_grad - delta)).astype(jnp.bfloat16)
    dquery_ref[...] = jnp.dot(key_t_ref[0], score_low, preferred_element_type=jnp.float32)
    dkey = jnp.dot(score_low, query_ref[...], preferred_element_type=jnp.float32)
    dvalue = jnp.dot(
        probs.astype(jnp.bfloat16), grad_ref[...], preferred_element_type=jnp.float32
    )
    first = lax.rem(step, tiles_first) == 0

    @pl.when(first)
    def _():
        dkey_ref[0] = dkey
        dvalue_ref[0] = dvalue

    @pl.when(jnp.logical_not(first))
    def _():
        dkey_ref[0] += dkey
        dvalue_ref[0] += dvalue


def attend_back(query, key, key_t, value, grad, out, grad_t, lse):
    rows, keys = query.shape[0], key.shape[1]
    tiles_first = keys // QTILE
    pair = lambda i: (i // tiles_first, 0, 0)
    return pl.pallas_call(
        functools.partial(attend_back_kernel, tiles_first),
        grid=(rows // QTILE,),
        in_specs=[
            pl.BlockSpec((QTILE, 2 * HEAD_DIM), lambda i: (i, 0)),
            pl.BlockSpec((1, keys, 2 * HEAD_DIM), pair),
            pl.BlockSpec((1, HEAD_DIM, keys), pair),
            pl.BlockSpec((1, keys, HEAD_DIM), pair),
            pl.BlockSpec((QTILE, HEAD_DIM), lambda i: (i, 0)),
            pl.BlockSpec((HEAD_DIM, QTILE), lambda i: (0, i)),
            pl.BlockSpec((HEAD_DIM, QTILE), lambda i: (0, i)),
            pl.BlockSpec((1, QTILE), lambda i: (0, i)),
        ],
        out_specs=[
            pl.BlockSpec((HEAD_DIM, QTILE), lambda i: (0, i)),
            pl.BlockSpec((1, keys, 2 * HEAD_DIM), pair),
            pl.BlockSpec((1, keys, HEAD_DIM), pair),
        ],
        out_shape=[
            jax.ShapeDtypeStruct((HEAD_DIM, rows), jnp.float32),
            jax.ShapeDtypeStruct((2, keys, 2 * HEAD_DIM), jnp.float32),
            jax.ShapeDtypeStruct((2, keys, HEAD_DIM), jnp.float32),
        ],
        compiler_params=pltpu.CompilerParams(vmem_limit_bytes=52 << 20),
        cost_estimate=pl.CostEstimate(
            flops=10 * rows * keys * HEAD_DIM, bytes_accessed=12 << 20, transcendentals=rows * keys
        ),
    )(query, key, key_t, value, grad, out, grad_t, lse)


def pick_heads(columns, heads):
    return jnp.concatenate([columns[:, h * HEAD_DIM : (h + 1) * HEAD_DIM] for h in heads], axis=1)


def unit_heads(target):
    return 3 * (target // 2) + target % 2, 3 * (target // 2) + 2


def dealt_forward(packed, block_table, seq_length, n_ctx):
    rows = packed.shape[0]
    half = n_ctx // 2 * rows
    core = lax.axis_index("ctx") % 2
    sends = []
    for target in range(n_ctx):
        whole, shared = unit_heads(target)
        sends.append(
            pick_heads(
                packed,
                [whole, HEADS + whole, 2 * HEADS + whole, shared, HEADS + shared, 2 * HEADS + shared],
            )
        )
    got = exchange(jnp.stack(sends), "ctx", 1).reshape(n_ctx * rows, 6, HEAD_DIM)
    total = n_ctx * rows
    valid = key_valid(0, total, BLK, block_table, seq_length)
    mask_col = jnp.where(valid, 0.0, NEG_FILL).astype(jnp.bfloat16)[:, None]
    query = jnp.concatenate(
        [got[:, 0], lax.dynamic_slice_in_dim(got[:, 3], core * half, half, axis=0)], axis=0
    ) * jnp.bfloat16(1.0 / math.sqrt(HEAD_DIM))
    ones_col = jnp.ones((query.shape[0], 1), jnp.bfloat16)
    query = jnp.concatenate(
        [query, ones_col, jnp.zeros((query.shape[0], HEAD_DIM - 1), jnp.bfloat16)], axis=1
    )
    fill = jnp.zeros((total, HEAD_DIM - 1), jnp.bfloat16)
    key = jnp.stack(
        [
            jnp.concatenate([got[:, 1], mask_col, fill], axis=1),
            jnp.concatenate([got[:, 4], mask_col, fill], axis=1),
        ]
    )
    value = jnp.stack([got[:, 2], got[:, 5]])
    out, lse = attend(query, key, jnp.swapaxes(value, 1, 2))
    low = jnp.transpose(out.astype(jnp.bfloat16))
    first = low[:total].reshape(n_ctx, rows, HEAD_DIM)
    second = lax.dynamic_update_slice_in_dim(
        jnp.zeros((total, HEAD_DIM), jnp.bfloat16), low[total:], core * half, axis=0
    ).reshape(n_ctx, rows, HEAD_DIM)
    back = exchange(jnp.concatenate([first, second], axis=2), "ctx", 2)
    upper = lax.axis_index("ctx") >= n_ctx // 2
    pieces = []
    for chip in range(n_ctx // 2):
        pieces += [
            back[2 * chip, :, :HEAD_DIM],
            back[2 * chip + 1, :, :HEAD_DIM],
            jnp.where(upper, back[2 * chip + 1, :, HEAD_DIM:], back[2 * chip, :, HEAD_DIM:]),
        ]
    return jnp.concatenate(pieces, axis=1), (query, key, value, out, lse)


def dealt_backward(context_grad, saved, n_ctx):
    query, key, value, out, lse = saved
    rows = context_grad.shape[0]
    total = n_ctx * rows
    half = total // 2
    core = lax.axis_index("ctx") % 2
    sends = jnp.stack([pick_heads(context_grad, unit_heads(target)) for target in range(n_ctx)])
    got = exchange(sends, "ctx", 3).reshape(total, 2 * HEAD_DIM)
    grad = jnp.concatenate(
        [
            got[:, :HEAD_DIM],
            lax.dynamic_slice_in_dim(got[:, HEAD_DIM:], core * half, half, axis=0),
        ],
        axis=0,
    )
    key_t = jnp.swapaxes(key[:, :, :HEAD_DIM], 1, 2)
    dquery_t, dkey, dvalue = attend_back(
        query, key, key_t, value, grad, out, jnp.transpose(grad), lse
    )
    dquery = jnp.transpose((dquery_t * (1.0 / math.sqrt(HEAD_DIM))).astype(jnp.bfloat16))
    dkey = dkey[:, :, :HEAD_DIM].astype(jnp.bfloat16)
    dvalue = dvalue.astype(jnp.bfloat16)
    dshared = lax.dynamic_update_slice_in_dim(
        jnp.zeros((total, HEAD_DIM), jnp.bfloat16), dquery[total:], core * half, axis=0
    )
    sends = jnp.concatenate(
        [dquery[:total], dkey[0], dvalue[0], dshared, dkey[1], dvalue[1]], axis=1
    ).reshape(n_ctx, rows, 6 * HEAD_DIM)
    back = exchange(sends, "ctx", 4)
    piece = lambda source, k: back[source, :, k * HEAD_DIM : (k + 1) * HEAD_DIM]
    both = lambda chip, k: (
        piece(2 * chip, k).astype(jnp.float32) + piece(2 * chip + 1, k).astype(jnp.float32)
    ).astype(jnp.bfloat16)
    queries, keys, values = [], [], []
    for chip in range(n_ctx // 2):
        queries += [piece(2 * chip, 0), piece(2 * chip + 1, 0), both(chip, 3)]
        keys += [piece(2 * chip, 1), piece(2 * chip + 1, 1), both(chip, 4)]
        values += [piece(2 * chip, 2), piece(2 * chip + 1, 2), both(chip, 5)]
    return jnp.concatenate(queries + keys + values, axis=1)


def scan_forward(packed, block_table, seq_length):
    feat_width = HEADS * HEAD_DIM
    tok_rows = packed.shape[0]
    blk_rows = BLK
    score_scale = 1.0 / math.sqrt(HEAD_DIM)
    query_heads = packed[:, :feat_width].reshape(tok_rows, HEADS, HEAD_DIM)
    key_rows = packed[:, feat_width : 2 * feat_width]
    value_rows = packed[:, 2 * feat_width :]
    start_state = (
        jnp.full((HEADS, tok_rows), NEG_FILL, jnp.float32),
        jnp.zeros((HEADS, tok_rows), jnp.float32),
        jnp.zeros((tok_rows, HEADS, HEAD_DIM), jnp.float32),
    )
    key_piece = lax.all_gather(key_rows, "ctx", axis=0, tiled=True)
    value_piece = lax.all_gather(value_rows, "ctx", axis=0, tiled=True)
    piece_rows = key_piece.shape[0]
    fold_blk_size = math.gcd(piece_rows, 1024)
    num_blocks = piece_rows // fold_blk_size
    key_blocks = key_piece.reshape(num_blocks, fold_blk_size, HEADS, HEAD_DIM)
    value_blocks = value_piece.reshape(num_blocks, fold_blk_size, HEADS, HEAD_DIM)
    offsets = fold_blk_size * jnp.arange(num_blocks, dtype=jnp.int32)

    def scan_step(state_in, loop_item):
        running_max, running_sum, accum_out = state_in
        key_blk, value_blk, offset = loop_item
        valid_keys = key_valid(offset, fold_blk_size, blk_rows, block_table, seq_length)
        scores = (
            jnp.einsum("qhd,khd->hqk", query_heads, key_blk, preferred_element_type=jnp.float32)
            * score_scale
        )
        scores = jnp.where(valid_keys[None, None, :], scores, NEG_FILL)
        new_max = jnp.maximum(running_max, jnp.max(scores, axis=2))
        factor = jnp.exp(running_max - new_max)
        soft_weights = jnp.exp(scores - new_max[:, :, None])
        new_sum = running_sum * factor + jnp.sum(soft_weights, axis=2)
        update = jnp.einsum(
            "hqk,khd->qhd",
            soft_weights.astype(jnp.bfloat16),
            value_blk,
            preferred_element_type=jnp.float32,
        )
        accum_out = accum_out * jnp.transpose(factor)[:, :, None] + update
        return ((new_max, new_sum, accum_out), None)

    result, _ = lax.scan(scan_step, start_state, (key_blocks, value_blocks, offsets))
    run_max, run_sum, accum_out = result
    lse = run_max + jnp.log(run_sum)
    attn_heads = accum_out / jnp.transpose(run_sum)[:, :, None]
    context = attn_heads.reshape(tok_rows, feat_width).astype(jnp.bfloat16)
    return context, (query_heads, key_rows, value_rows, lse, attn_heads)


def scan_backward(context_grad, saved, block_table, seq_length):
    query_heads, key_rows, value_rows, lse, attn_heads = saved
    feat_width = HEADS * HEAD_DIM
    tok_rows = context_grad.shape[0]
    blk_rows = BLK
    score_scale = 1.0 / math.sqrt(HEAD_DIM)
    grad_heads = context_grad.reshape(tok_rows, HEADS, HEAD_DIM)
    delta = jnp.einsum("qhd,qhd->hq", grad_heads.astype(jnp.float32), attn_heads)
    gathered_keys, gathered_values = (
        lax.all_gather(key_rows, "ctx", axis=0, tiled=True),
        lax.all_gather(value_rows, "ctx", axis=0, tiled=True),
    )
    total_rows = gathered_keys.shape[0]
    blk_size = math.gcd(total_rows, 1024)
    num_blocks = total_rows // blk_size
    key_blocks = gathered_keys.reshape(num_blocks, blk_size, HEADS, HEAD_DIM)
    value_blocks = gathered_values.reshape(num_blocks, blk_size, HEADS, HEAD_DIM)
    offsets = blk_size * jnp.arange(num_blocks, dtype=jnp.int32)

    def scan_back(query_acc, loop_item):
        key_blk, value_blk, offset = loop_item
        valid_keys = key_valid(offset, blk_size, blk_rows, block_table, seq_length)
        attn_probs = exp_scores(query_heads, key_blk, valid_keys, lse, score_scale)
        value_part = jnp.einsum(
            "hqk,qhd->khd",
            attn_probs.astype(jnp.bfloat16),
            grad_heads,
            preferred_element_type=jnp.float32,
        )
        prob_grad = jnp.einsum(
            "qhd,khd->hqk", grad_heads, value_blk, preferred_element_type=jnp.float32
        )
        score_low = (attn_probs * (prob_grad - delta[:, :, None])).astype(jnp.bfloat16)
        query_acc = (
            query_acc
            + jnp.einsum("hqk,khd->qhd", score_low, key_blk, preferred_element_type=jnp.float32)
            * score_scale
        )
        key_part = (
            jnp.einsum("hqk,qhd->khd", score_low, query_heads, preferred_element_type=jnp.float32)
            * score_scale
        )
        return (
            query_acc,
            jnp.concatenate(
                [key_part.reshape(blk_size, feat_width), value_part.reshape(blk_size, feat_width)],
                axis=1,
            ),
        )

    query_acc, terms = lax.scan(
        scan_back,
        jnp.zeros((tok_rows, HEADS, HEAD_DIM), jnp.float32),
        (key_blocks, value_blocks, offsets),
    )
    key_value_grad = lax.psum_scatter(
        terms.reshape(total_rows, 2 * feat_width), "ctx", scatter_dimension=0, tiled=True
    )
    query_grad = query_acc.reshape(tok_rows, feat_width)
    key_grad = key_value_grad[:, :feat_width]
    value_grad = key_value_grad[:, feat_width:]
    return jnp.concatenate([query_grad, key_grad, value_grad], axis=1).astype(jnp.bfloat16)


def core_pairs(n_ctx):
    return [[2 * z, 2 * z + 1] for z in range(n_ctx // 2)]


def core_columns(n_ctx):
    return [list(range(0, n_ctx, 2)), list(range(1, n_ctx, 2))]


def gather_weight(shard, n_ctx):
    rows, columns = shard.shape
    half = rows // 2
    core = lax.axis_index("ctx") % 2
    mine = lax.dynamic_slice_in_dim(shard, core * half, half, axis=0)
    quarter = lax.all_gather(mine, "fsdp", axis=0)
    whole = lax.all_gather(quarter, "ctx", axis=1, axis_index_groups=core_pairs(n_ctx))
    return whole.reshape(-1, columns)


def reduce_weight(grad, n_fsdp, n_ctx):
    rows, columns = grad.shape
    if n_ctx != 8:
        part = lax.psum_scatter(
            grad.astype(jnp.bfloat16), "fsdp", scatter_dimension=0, tiled=True
        ).astype(jnp.float32)
        return lax.psum(part, "ctx")
    piece = rows // (n_fsdp * n_ctx)
    low = grad.astype(jnp.bfloat16).reshape(n_fsdp, n_ctx // 2, 2, piece, columns)
    low = lax.psum_scatter(
        low, "ctx", scatter_dimension=2, axis_index_groups=core_pairs(n_ctx)
    )
    low = lax.psum_scatter(low, "fsdp", scatter_dimension=0)
    low = lax.psum_scatter(
        low, "ctx", scatter_dimension=0, axis_index_groups=core_columns(n_ctx)
    )
    whole = lax.all_gather(low, "ctx", axis=0, tiled=True)
    return whole.astype(jnp.float32)


def local(
    tokens,
    cotangent,
    lengths,
    block_table,
    qkv_weight,
    query_bias,
    value_bias,
    proj_weight,
    proj_bias,
    gain_first,
    shift_first,
    inner_weight,
    inner_bias,
    outer_weight,
    outer_bias,
    gain_second,
    shift_second,
):
    feat_width = HEADS * HEAD_DIM
    tok_rows = tokens.shape[0]
    seq_length = lengths[0]
    n_fsdp = lax.axis_size("fsdp")
    n_ctx = lax.axis_size("ctx")
    dealt = n_ctx == 8 and tok_rows == 256
    vectors = (
        query_bias,
        value_bias,
        proj_bias,
        gain_first,
        shift_first,
        inner_bias,
        outer_bias,
        gain_second,
        shift_second,
    )
    ends = [0]
    for vector in vectors:
        ends.append(ends[-1] + vector.shape[0])
    gathered = lax.all_gather(jnp.concatenate(vectors)[None], "fsdp", axis=0, tiled=True)
    (
        qbias_full,
        vbias_full,
        pbias_full,
        gain1_full,
        shift1_full,
        ibias_full,
        obias_full,
        gain2_full,
        shift2_full,
    ) = [gathered[:, ends[k] : ends[k + 1]].reshape(-1) for k in range(len(vectors))]
    qkv_full = gather_weight(qkv_weight, n_ctx)
    proj_full = gather_weight(proj_weight, n_ctx)
    inner_full = gather_weight(inner_weight, n_ctx)
    outer_full = gather_weight(outer_weight, n_ctx)
    tokens_wide = tokens.astype(jnp.float32)
    bias_row = jnp.concatenate([qbias_full, jnp.zeros_like(qbias_full), vbias_full]).astype(
        jnp.float32
    )
    packed = (jnp.dot(tokens, qkv_full, preferred_element_type=jnp.float32) + bias_row).astype(
        jnp.bfloat16
    )
    if dealt:
        context, saved = dealt_forward(packed, block_table, seq_length, n_ctx)
    else:
        context, saved = scan_forward(packed, block_table, seq_length)
    hidden = (
        tokens_wide
        + jnp.dot(context, proj_full, preferred_element_type=jnp.float32)
        + pbias_full.astype(jnp.float32)
    )
    normed, norm_back = jax.vjp(
        layer_norm, hidden, gain1_full.astype(jnp.float32), shift1_full.astype(jnp.float32)
    )
    normed_low = normed.astype(jnp.bfloat16)
    inner_pre = jnp.dot(
        normed_low, inner_full, preferred_element_type=jnp.float32
    ) + ibias_full.astype(jnp.float32)
    active, gelu_back = jax.vjp(gelu_exact, inner_pre)
    active_low = active.astype(jnp.bfloat16)
    mixed_sum = (
        normed
        + jnp.dot(active_low, outer_full, preferred_element_type=jnp.float32)
        + obias_full.astype(jnp.float32)
    )
    result, final_back = jax.vjp(
        layer_norm, mixed_sum, gain2_full.astype(jnp.float32), shift2_full.astype(jnp.float32)
    )
    layer_out = result.astype(jnp.bfloat16)
    mixed_grad, gain2_grad, shift2_grad = final_back(cotangent.astype(jnp.float32))
    branch_low = mixed_grad.astype(jnp.bfloat16)
    outer_grad = cross_dot(active_low, branch_low)
    obias_grad = jnp.sum(branch_low.astype(jnp.float32), axis=0)
    (inner_grad_wide,) = gelu_back(back_dot(branch_low, outer_full))
    inner_low = inner_grad_wide.astype(jnp.bfloat16)
    inner_grad = cross_dot(normed_low, inner_low)
    ibias_grad = jnp.sum(inner_low.astype(jnp.float32), axis=0)
    normed_grad = mixed_grad + back_dot(inner_low, inner_full)
    hidden_grad, gain1_grad, shift1_grad = norm_back(normed_grad)
    proj_low = hidden_grad.astype(jnp.bfloat16)
    proj_grad = cross_dot(context, proj_low)
    pbias_grad = jnp.sum(proj_low.astype(jnp.float32), axis=0)
    context_grad = back_dot(proj_low, proj_full).astype(jnp.bfloat16)
    if dealt:
        packed_grad = dealt_backward(context_grad, saved, n_ctx)
    else:
        packed_grad = scan_backward(context_grad, saved, block_table, seq_length)
    qkv_grad = cross_dot(tokens, packed_grad)
    qbias_grad = jnp.sum(packed_grad[:, :feat_width].astype(jnp.float32), axis=0)
    vbias_grad = jnp.sum(packed_grad[:, 2 * feat_width :].astype(jnp.float32), axis=0)
    tokens_grad = (hidden_grad + back_dot(packed_grad, qkv_full)).astype(jnp.bfloat16)
    sums = (
        qbias_grad,
        vbias_grad,
        pbias_grad,
        gain1_grad,
        shift1_grad,
        ibias_grad,
        obias_grad,
        gain2_grad,
        shift2_grad,
    )
    bundle = jnp.concatenate([total.reshape(n_fsdp, -1) for total in sums], axis=1)
    bundle = lax.psum(bundle, ("fsdp", "ctx"))
    bundle = lax.dynamic_index_in_dim(bundle, lax.axis_index("fsdp"), axis=0, keepdims=False)
    vector_parts = [bundle[ends[k] : ends[k + 1]] for k in range(len(sums))]
    return (
        layer_out,
        tokens_grad,
        reduce_weight(qkv_grad, n_fsdp, n_ctx),
        vector_parts[0],
        vector_parts[1],
        reduce_weight(proj_grad, n_fsdp, n_ctx),
        vector_parts[2],
        vector_parts[3],
        vector_parts[4],
        reduce_weight(inner_grad, n_fsdp, n_ctx),
        vector_parts[5],
        reduce_weight(outer_grad, n_fsdp, n_ctx),
        vector_parts[6],
        vector_parts[7],
        vector_parts[8],
    )


def solution(mesh):
    placed = (
        P(("fsdp", "ctx"), None),
        P(("fsdp", "ctx"), None),
        P("fsdp"),
        P(),
        P("fsdp", None),
        P("fsdp"),
        P("fsdp"),
        P("fsdp", None),
        P("fsdp"),
        P("fsdp"),
        P("fsdp"),
        P("fsdp", None),
        P("fsdp"),
        P("fsdp", None),
        P("fsdp"),
        P("fsdp"),
        P("fsdp"),
    )
    return jax.shard_map(
        local,
        mesh=mesh,
        in_specs=placed,
        out_specs=(
            P(("fsdp", "ctx"), None),
            P(("fsdp", "ctx"), None),
            P("fsdp", None),
            P("fsdp"),
            P("fsdp"),
            P("fsdp", None),
            P("fsdp"),
            P("fsdp"),
            P("fsdp"),
            P("fsdp", None),
            P("fsdp"),
            P("fsdp", None),
            P("fsdp"),
            P("fsdp"),
            P("fsdp"),
        ),
        check_vma=False,
    )
```

```python
import functools
import math

import jax
import jax.numpy as jnp
from jax import lax
from jax.experimental import pallas as pl
from jax.experimental.pallas import tpu as pltpu
from jax.sharding import PartitionSpec as P

HEADS = 12
HEAD_DIM = 64
BLK = 128


NEG_FILL = -1e30
NORM_EPS = 1e-05


def layer_norm(vector_in, gain_in, shift_in):
    center = vector_in - jnp.mean(vector_in, axis=-1, keepdims=True)
    spread = jnp.mean(center * center, axis=-1, keepdims=True)
    return center * lax.rsqrt(spread + NORM_EPS) * gain_in + shift_in


def gelu_exact(vector_in):
    return jax.nn.gelu(vector_in, approximate=False)


def cross_dot(first_op, second_op):
    return lax.dot_general(
        first_op, second_op, (((0,), (0,)), ((), ())), preferred_element_type=jnp.float32
    )


def back_dot(first_op, second_op):
    return lax.dot_general(
        first_op, second_op, (((1,), (1,)), ((), ())), preferred_element_type=jnp.float32
    )


def key_valid(start_row, piece_rows, blk_rows, block_table, seq_length):
    index_rows = start_row + jnp.arange(piece_rows, dtype=jnp.int32)
    owner_block = index_rows // blk_rows
    table_slots = jnp.arange(block_table.shape[0], dtype=jnp.int32)
    placed = jnp.sum(
        jnp.where(owner_block[:, None] == table_slots[None, :], block_table[None, :], 0), axis=1
    )
    return placed * blk_rows + index_rows % blk_rows < seq_length


def exp_scores(query_blk, key_blk, valid_keys, lse_blk, score_scale):
    scores = (
        jnp.einsum("qhd,khd->hqk", query_blk, key_blk, preferred_element_type=jnp.float32)
        * score_scale
    )
    scores = jnp.where(valid_keys[None, None, :], scores, NEG_FILL)
    return jnp.exp(scores - lse_blk[:, :, None])


MESH_IDS = pl.DeviceIdType.MESH


def beside():
    f = lax.axis_index("fsdp")
    c = lax.axis_index("ctx")
    x, y = lax.rem(f, 2), f // 2
    core = lax.rem(c, 2)
    over_x = 2 * y + (1 - x)
    over_y = 2 * (1 - y) + x
    over_both = 2 * (1 - y) + (1 - x)
    return f, over_x, over_y, over_both, core, c + 1 - 2 * core


def greet(targets):
    barrier = pltpu.get_barrier_semaphore()
    for target in targets:
        pl.semaphore_signal(barrier, inc=1, device_id=target, device_id_type=MESH_IDS)
    pl.semaphore_wait(barrier, len(targets))


def remote(source, target, send, recv, device):
    return pltpu.make_async_remote_copy(
        src_ref=source,
        dst_ref=target,
        send_sem=send,
        recv_sem=recv,
        device_id=device,
        device_id_type=MESH_IDS,
    )


class Swap:
    def __init__(self, n, x_ref, y_ref, send_sem, recv_sem, own_sem):
        self.n, self.x_ref, self.y_ref = n, x_ref, y_ref
        self.send_sem, self.recv_sem, self.own_sem = send_sem, recv_sem, own_sem
        self.me = lax.axis_index("ctx")
        self.own = pltpu.make_async_copy(x_ref.at[self.me], y_ref.at[self.me], own_sem)

    def targets(self):
        return [{"ctx": lax.rem(self.me + step, self.n)} for step in range(1, self.n)]

    def start(self):
        self.own.start()
        for step in range(1, self.n):
            peer = lax.rem(self.me + step, self.n)
            remote(
                self.x_ref.at[peer],
                self.y_ref.at[self.me],
                self.send_sem.at[step],
                self.recv_sem.at[step],
                {"ctx": peer},
            ).start()

    def finish(self):
        self.own.wait()
        for step in range(1, self.n):
            source = lax.rem(self.me + self.n - step, self.n)
            remote(
                self.x_ref.at[source],
                self.y_ref.at[source],
                self.send_sem.at[step],
                self.recv_sem.at[step],
                {"ctx": source},
            ).wait()


class Gather:
    def __init__(self, w_ref, o_ref, send_sem, recv_sem, own_sem):
        self.w_ref, self.o_ref = w_ref, o_ref
        self.f, self.fx, self.fy, self.fd, self.core, self.sibling = beside()
        half = w_ref.shape[1] // 2
        upper, lower = pl.ds(0, half), pl.ds(half, half)
        f, fx, fy, fd, k = self.f, self.fx, self.fy, self.fd, self.core
        to_x, to_y, to_core = {"fsdp": fx}, {"fsdp": fy}, {"ctx": self.sibling}
        o = o_ref

        def copy(number, source, target, device):
            return remote(source, target, send_sem.at[number], recv_sem.at[number], device)

        self.own = pltpu.make_async_copy(w_ref, o.at[f], own_sem)
        self.sends = [
            copy(0, w_ref.at[k], o.at[f, k], to_x),
            copy(1, w_ref.at[k], o.at[f, k], to_y),
            copy(2, o.at[fx, k, upper], o.at[fx, k, upper], to_y),
            copy(3, o.at[fx, k], o.at[fx, k], to_core),
            copy(4, o.at[fy, k, lower], o.at[fy, k, lower], to_x),
            copy(5, o.at[fy, k], o.at[fy, k], to_core),
            copy(6, o.at[fd, k], o.at[fd, k], to_core),
        ]
        other = 1 - k
        self.takes = [
            copy(0, w_ref.at[k], o.at[fx, k], to_x),
            copy(1, w_ref.at[k], o.at[fy, k], to_y),
            copy(2, o.at[fd, k, upper], o.at[fd, k, upper], to_y),
            copy(3, o.at[fx, other], o.at[fx, other], to_core),
            copy(4, o.at[fd, k, lower], o.at[fd, k, lower], to_x),
            copy(5, o.at[fy, other], o.at[fy, other], to_core),
            copy(6, o.at[fd, other], o.at[fd, other], to_core),
        ]

    def targets(self):
        return [{"fsdp": self.fx}, {"fsdp": self.fy}]

    def start(self):
        self.sends[0].start()
        self.sends[1].start()
        self.own.start()

    def finish(self):
        self.takes[0].wait_recv()
        self.sends[2].start()
        self.sends[3].start()
        self.takes[1].wait_recv()
        self.sends[4].start()
        self.sends[5].start()
        self.takes[2].wait_recv()
        self.takes[4].wait_recv()
        self.sends[6].start()
        for number in (3, 5, 6):
            self.takes[number].wait_recv()
        self.own.wait()
        for send in self.sends:
            send.wait_send()


def swap_kernel(n, x_ref, y_ref, *sems):
    swap = Swap(n, x_ref, y_ref, *sems)
    greet(swap.targets())
    swap.start()
    swap.finish()


def gather_kernel(w_ref, o_ref, *sems):
    gather = Gather(w_ref, o_ref, *sems)
    greet(gather.targets() + [{"ctx": gather.sibling}])
    gather.start()
    gather.finish()


def swap_gather_kernel(n, x_ref, w_ref, y_ref, o_ref, *sems):
    swap = Swap(n, x_ref, y_ref, *sems[:3])
    gather = Gather(w_ref, o_ref, *sems[3:])
    greet(swap.targets() + gather.targets())
    gather.start()
    swap.start()
    gather.finish()
    swap.finish()


def vmem_specs(count):
    return [pl.BlockSpec(memory_space=pltpu.VMEM)] * count


def copy_sems(count):
    return [
        pltpu.SemaphoreType.DMA((count,)),
        pltpu.SemaphoreType.DMA((count,)),
        pltpu.SemaphoreType.DMA,
    ]


def linked(number, limit):
    return pltpu.CompilerParams(
        collective_id=number, has_side_effects=True, vmem_limit_bytes=limit << 20
    )


def exchange(blocks, number):
    n = blocks.shape[0]
    return pl.pallas_call(
        functools.partial(swap_kernel, n),
        out_shape=jax.ShapeDtypeStruct(blocks.shape, blocks.dtype),
        in_specs=vmem_specs(1),
        out_specs=vmem_specs(1)[0],
        scratch_shapes=copy_sems(n),
        compiler_params=linked(number, 16),
    )(blocks)


def gather_kernel_call(shard, number):
    rows, columns = shard.shape
    whole = pl.pallas_call(
        gather_kernel,
        out_shape=jax.ShapeDtypeStruct((4, 2, rows // 2, columns), shard.dtype),
        in_specs=vmem_specs(1),
        out_specs=vmem_specs(1)[0],
        scratch_shapes=copy_sems(7),
        compiler_params=linked(number, 16),
    )(shard.reshape(2, rows // 2, columns))
    return whole.reshape(4 * rows, columns)


def exchange_gather(blocks, shard, number):
    n = blocks.shape[0]
    rows, columns = shard.shape
    swapped, whole = pl.pallas_call(
        functools.partial(swap_gather_kernel, n),
        out_shape=[
            jax.ShapeDtypeStruct(blocks.shape, blocks.dtype),
            jax.ShapeDtypeStruct((4, 2, rows // 2, columns), shard.dtype),
        ],
        in_specs=vmem_specs(2),
        out_specs=vmem_specs(2),
        scratch_shapes=copy_sems(n) + copy_sems(7),
        compiler_params=linked(number, 24),
    )(blocks, shard.reshape(2, rows // 2, columns))
    return swapped, whole.reshape(4 * rows, columns)


CHUNKS = 3


def wide_sum(*parts):
    total = parts[0].astype(jnp.float32)
    for part in parts[1:]:
        total = total + part.astype(jnp.float32)
    return total.astype(jnp.bfloat16)


def reduce_kernel(*refs):
    ins, outs = refs[:CHUNKS], refs[CHUNKS : 2 * CHUNKS]
    halves, side, turn, deep, send_sem, recv_sem = refs[2 * CHUNKS :]
    f, fx, fy, _, k, sibling = beside()
    c = lax.axis_index("ctx")
    z = c // 2
    x, y = lax.rem(f, 2), f // 2
    to_x, to_y, to_core = {"fsdp": fx}, {"fsdp": fy}, {"ctx": sibling}
    depth = [lax.rem(z + step, 4) for step in range(1, 4)]
    source = [lax.rem(z + 4 - step, 4) for step in range(1, 4)]
    to_z = [{"ctx": 2 * peer + k} for peer in depth]
    low, high = pl.ds(0, 2), pl.ds(2, 2)

    def copy(j, number, origin, target, device):
        return remote(origin, target, send_sem.at[j, number], recv_sem.at[j, number], device)

    def core_copies(j):
        return [
            copy(j, g, ins[j].at[g, 1 - k], halves.at[j, g], to_core) for g in range(4)
        ]

    def side_copies(j):
        copies = []
        for t in range(2):
            goes = 2 * t + (1 - x)
            copies.append(copy(j, 4 + t, halves.at[j, goes, low], side.at[j, t], to_x))
            goes = 2 * (1 - y) + t
            copies.append(copy(j, 6 + t, halves.at[j, goes, high], side.at[j, 2 + t], to_y))
        return copies

    def turn_copies(j):
        return [
            copy(j, 8, halves.at[j, fy, low], turn.at[j, 0], to_y),
            copy(j, 9, halves.at[j, fx, high], turn.at[j, 1], to_x),
        ]

    def deep_copies(j):
        return [
            copy(j, 10 + i, halves.at[j, f, depth[i]], deep.at[j, i], to_z[i]) for i in range(3)
        ]

    def back_copies(j):
        return [copy(j, 13 + i, outs[j].at[k, z], outs[j].at[k, z], to_z[i]) for i in range(3)]

    def back_takes(j):
        return [
            copy(j, 13 + i, outs[j].at[k, source[i]], outs[j].at[k, source[i]], to_z[i])
            for i in range(3)
        ]

    def last_copy(j):
        return copy(j, 16, outs[j].at[k], outs[j].at[k], to_core)

    def last_take(j):
        return copy(j, 16, outs[j].at[1 - k], outs[j].at[1 - k], to_core)

    def start_all(copies):
        for one in copies:
            one.start()

    def take_all(copies):
        for one in copies:
            one.wait_recv()

    def phase_core(j):
        take_all(core_copies(j))

        @pl.loop(0, 16)
        def _(i):
            g, d = i // 4, lax.rem(i, 4)
            halves[j, g, d] = wide_sum(halves[j, g, d], ins[j][g, k, d])

        start_all(side_copies(j))

    def phase_side(j):
        copies = side_copies(j)
        for one in copies:
            one.wait()

        @pl.loop(0, 2)
        def _(d):
            for t in range(2):
                keeps = 2 * t + x
                halves[j, keeps, d] = wide_sum(halves[j, keeps, d], side[j, t, d])
                keeps = 2 * y + t
                halves[j, keeps, 2 + d] = wide_sum(halves[j, keeps, 2 + d], side[j, 2 + t, d])

        start_all(turn_copies(j))

    def phase_turn(j):
        for one in turn_copies(j):
            one.wait()

        @pl.loop(0, 2)
        def _(d):
            halves[j, f, d] = wide_sum(halves[j, f, d], turn[j, 0, d])
            halves[j, f, 2 + d] = wide_sum(halves[j, f, 2 + d], turn[j, 1, d])

        start_all(deep_copies(j))

    def phase_deep(j):
        take_all(deep_copies(j))
        outs[j][k, z] = wide_sum(halves[j, f, z], deep[j, 0], deep[j, 1], deep[j, 2])
        start_all(back_copies(j))

    def phase_back(j):
        take_all(back_takes(j))
        last_copy(j).start()

    def phase_last(j):
        last_take(j).wait_recv()
        for one in core_copies(j) + deep_copies(j) + back_copies(j) + [last_copy(j)]:
            one.wait_send()

    greet([to_x, to_y, to_core] + to_z)
    for j in range(CHUNKS):
        start_all(core_copies(j))
    phases = [phase_core, phase_side, phase_turn, phase_deep, phase_back, phase_last]
    for tick in range(CHUNKS + len(phases) - 1):
        for order in reversed(range(len(phases))):
            if 0 <= tick - order < CHUNKS:
                phases[order](tick - order)


def reduce_grads(chunks):
    count, rows, width = chunks[0].shape
    piece = rows // 8
    shaped = [chunk.reshape(4, 2, 4, piece, width) for chunk in chunks]
    low = jnp.bfloat16
    outs = pl.pallas_call(
        reduce_kernel,
        out_shape=[jax.ShapeDtypeStruct((2, 4, piece, width), low)] * CHUNKS,
        in_specs=vmem_specs(CHUNKS),
        out_specs=vmem_specs(CHUNKS),
        scratch_shapes=[
            pltpu.VMEM((CHUNKS, 4, 4, piece, width), low),
            pltpu.VMEM((CHUNKS, 4, 2, piece, width), low),
            pltpu.VMEM((CHUNKS, 2, 2, piece, width), low),
            pltpu.VMEM((CHUNKS, 3, piece, width), low),
            pltpu.SemaphoreType.DMA((CHUNKS, 17)),
            pltpu.SemaphoreType.DMA((CHUNKS, 17)),
        ],
        compiler_params=linked(6, 48),
    )(*shaped)
    return [out.reshape(rows, width).astype(jnp.float32) for out in outs]


def split_wide(grad):
    rows, columns = grad.shape
    feat_width = HEADS * HEAD_DIM
    parts = grad.reshape(4, rows // 4, columns // feat_width, feat_width)
    return jnp.swapaxes(parts, 1, 2).reshape(4, -1, feat_width)


def join_wide(shard, rows):
    parts = shard.reshape(-1, rows, shard.shape[1])
    return jnp.swapaxes(parts, 0, 1).reshape(rows, -1)


QTILE = 512


def attend_kernel(query_ref, key_ref, value_ref, out_ref, lse_ref):
    scores = lax.dot_general(
        key_ref[0], query_ref[...], (((1,), (1,)), ((), ())), preferred_element_type=jnp.float32
    )
    top = jnp.max(scores, axis=0, keepdims=True)
    weights = jnp.exp(scores - top)
    total = jnp.sum(weights, axis=0, keepdims=True)
    out = jnp.dot(value_ref[0], weights.astype(jnp.bfloat16), preferred_element_type=jnp.float32)
    out_ref[...] = out / total
    lse_ref[...] = top + jnp.log(total)


def attend(query, key, value_t):
    rows, keys = query.shape[0], key.shape[1]
    tiles_first = keys // QTILE
    return pl.pallas_call(
        attend_kernel,
        grid=(rows // QTILE,),
        in_specs=[
            pl.BlockSpec((QTILE, 2 * HEAD_DIM), lambda i: (i, 0)),
            pl.BlockSpec((1, keys, 2 * HEAD_DIM), lambda i: (i // tiles_first, 0, 0)),
            pl.BlockSpec((1, HEAD_DIM, keys), lambda i: (i // tiles_first, 0, 0)),
        ],
        out_specs=[
            pl.BlockSpec((HEAD_DIM, QTILE), lambda i: (0, i)),
            pl.BlockSpec((1, QTILE), lambda i: (0, i)),
        ],
        out_shape=[
            jax.ShapeDtypeStruct((HEAD_DIM, rows), jnp.float32),
            jax.ShapeDtypeStruct((1, rows), jnp.float32),
        ],
        compiler_params=pltpu.CompilerParams(vmem_limit_bytes=40 << 20),
        cost_estimate=pl.CostEstimate(
            flops=4 * rows * keys * HEAD_DIM, bytes_accessed=8 << 20, transcendentals=rows * keys
        ),
    )(query, key, value_t)


def attend_back_kernel(
    tiles_first,
    query_ref,
    key_ref,
    key_t_ref,
    value_ref,
    grad_ref,
    out_ref,
    grad_t_ref,
    lse_ref,
    dquery_ref,
    dkey_ref,
    dvalue_ref,
):
    step = pl.program_id(0)
    scores = back_dot(key_ref[0], query_ref[...])
    probs = jnp.exp(scores - lse_ref[...])
    delta = jnp.sum(out_ref[...] * grad_t_ref[...].astype(jnp.float32), axis=0, keepdims=True)
    prob_grad = back_dot(value_ref[0], grad_ref[...])
    score_low = (probs * (prob_grad - delta)).astype(jnp.bfloat16)
    dquery_ref[...] = jnp.dot(key_t_ref[0], score_low, preferred_element_type=jnp.float32)
    dkey = jnp.dot(score_low, query_ref[...], preferred_element_type=jnp.float32)
    dvalue = jnp.dot(
        probs.astype(jnp.bfloat16), grad_ref[...], preferred_element_type=jnp.float32
    )
    first = lax.rem(step, tiles_first) == 0

    @pl.when(first)
    def _():
        dkey_ref[0] = dkey
        dvalue_ref[0] = dvalue

    @pl.when(jnp.logical_not(first))
    def _():
        dkey_ref[0] += dkey
        dvalue_ref[0] += dvalue


def attend_back(query, key, key_t, value, grad, out, grad_t, lse):
    rows, keys = query.shape[0], key.shape[1]
    tiles_first = keys // QTILE
    pair = lambda i: (i // tiles_first, 0, 0)
    return pl.pallas_call(
        functools.partial(attend_back_kernel, tiles_first),
        grid=(rows // QTILE,),
        in_specs=[
            pl.BlockSpec((QTILE, 2 * HEAD_DIM), lambda i: (i, 0)),
            pl.BlockSpec((1, keys, 2 * HEAD_DIM), pair),
            pl.BlockSpec((1, HEAD_DIM, keys), pair),
            pl.BlockSpec((1, keys, HEAD_DIM), pair),
            pl.BlockSpec((QTILE, HEAD_DIM), lambda i: (i, 0)),
            pl.BlockSpec((HEAD_DIM, QTILE), lambda i: (0, i)),
            pl.BlockSpec((HEAD_DIM, QTILE), lambda i: (0, i)),
            pl.BlockSpec((1, QTILE), lambda i: (0, i)),
        ],
        out_specs=[
            pl.BlockSpec((HEAD_DIM, QTILE), lambda i: (0, i)),
            pl.BlockSpec((1, keys, 2 * HEAD_DIM), pair),
            pl.BlockSpec((1, keys, HEAD_DIM), pair),
        ],
        out_shape=[
            jax.ShapeDtypeStruct((HEAD_DIM, rows), jnp.float32),
            jax.ShapeDtypeStruct((2, keys, 2 * HEAD_DIM), jnp.float32),
            jax.ShapeDtypeStruct((2, keys, HEAD_DIM), jnp.float32),
        ],
        compiler_params=pltpu.CompilerParams(vmem_limit_bytes=52 << 20),
        cost_estimate=pl.CostEstimate(
            flops=10 * rows * keys * HEAD_DIM, bytes_accessed=12 << 20, transcendentals=rows * keys
        ),
    )(query, key, key_t, value, grad, out, grad_t, lse)


def pick_heads(columns, heads):
    return jnp.concatenate([columns[:, h * HEAD_DIM : (h + 1) * HEAD_DIM] for h in heads], axis=1)


def unit_heads(target):
    return 3 * (target // 2) + target % 2, 3 * (target // 2) + 2


def dealt_forward(packed, block_table, seq_length, n_ctx, inner_weight, outer_weight):
    rows = packed.shape[0]
    half = n_ctx // 2 * rows
    core = lax.axis_index("ctx") % 2
    sends = []
    for target in range(n_ctx):
        whole, shared = unit_heads(target)
        sends.append(
            pick_heads(
                packed,
                [whole, HEADS + whole, 2 * HEADS + whole, shared, HEADS + shared, 2 * HEADS + shared],
            )
        )
    got, inner_full = exchange_gather(jnp.stack(sends), inner_weight, 1)
    got = got.reshape(n_ctx * rows, 6, HEAD_DIM)
    total = n_ctx * rows
    valid = key_valid(0, total, BLK, block_table, seq_length)
    mask_col = jnp.where(valid, 0.0, NEG_FILL).astype(jnp.bfloat16)[:, None]
    query = jnp.concatenate(
        [got[:, 0], lax.dynamic_slice_in_dim(got[:, 3], core * half, half, axis=0)], axis=0
    ) * jnp.bfloat16(1.0 / math.sqrt(HEAD_DIM))
    ones_col = jnp.ones((query.shape[0], 1), jnp.bfloat16)
    query = jnp.concatenate(
        [query, ones_col, jnp.zeros((query.shape[0], HEAD_DIM - 1), jnp.bfloat16)], axis=1
    )
    fill = jnp.zeros((total, HEAD_DIM - 1), jnp.bfloat16)
    key = jnp.stack(
        [
            jnp.concatenate([got[:, 1], mask_col, fill], axis=1),
            jnp.concatenate([got[:, 4], mask_col, fill], axis=1),
        ]
    )
    value = jnp.stack([got[:, 2], got[:, 5]])
    out, lse = attend(query, key, jnp.swapaxes(value, 1, 2))
    low = jnp.transpose(out.astype(jnp.bfloat16))
    first = low[:total].reshape(n_ctx, rows, HEAD_DIM)
    second = lax.dynamic_update_slice_in_dim(
        jnp.zeros((total, HEAD_DIM), jnp.bfloat16), low[total:], core * half, axis=0
    ).reshape(n_ctx, rows, HEAD_DIM)
    back, outer_full = exchange_gather(
        jnp.concatenate([first, second], axis=2), outer_weight, 2
    )
    upper = lax.axis_index("ctx") >= n_ctx // 2
    pieces = []
    for chip in range(n_ctx // 2):
        pieces += [
            back[2 * chip, :, :HEAD_DIM],
            back[2 * chip + 1, :, :HEAD_DIM],
            jnp.where(upper, back[2 * chip + 1, :, HEAD_DIM:], back[2 * chip, :, HEAD_DIM:]),
        ]
    context = jnp.concatenate(pieces, axis=1)
    return context, (query, key, value, out, lse), inner_full, outer_full


def dealt_backward(context_grad, saved, n_ctx):
    query, key, value, out, lse = saved
    rows = context_grad.shape[0]
    total = n_ctx * rows
    half = total // 2
    core = lax.axis_index("ctx") % 2
    sends = jnp.stack([pick_heads(context_grad, unit_heads(target)) for target in range(n_ctx)])
    got = exchange(sends, 3).reshape(total, 2 * HEAD_DIM)
    grad = jnp.concatenate(
        [
            got[:, :HEAD_DIM],
            lax.dynamic_slice_in_dim(got[:, HEAD_DIM:], core * half, half, axis=0),
        ],
        axis=0,
    )
    key_t = jnp.swapaxes(key[:, :, :HEAD_DIM], 1, 2)
    dquery_t, dkey, dvalue = attend_back(
        query, key, key_t, value, grad, out, jnp.transpose(grad), lse
    )
    dquery = jnp.transpose((dquery_t * (1.0 / math.sqrt(HEAD_DIM))).astype(jnp.bfloat16))
    dkey = dkey[:, :, :HEAD_DIM].astype(jnp.bfloat16)
    dvalue = dvalue.astype(jnp.bfloat16)
    dshared = lax.dynamic_update_slice_in_dim(
        jnp.zeros((total, HEAD_DIM), jnp.bfloat16), dquery[total:], core * half, axis=0
    )
    sends = jnp.concatenate(
        [dquery[:total], dkey[0], dvalue[0], dshared, dkey[1], dvalue[1]], axis=1
    ).reshape(n_ctx, rows, 6 * HEAD_DIM)
    back = exchange(sends, 4)
    piece = lambda source, k: back[source, :, k * HEAD_DIM : (k + 1) * HEAD_DIM]
    both = lambda chip, k: (
        piece(2 * chip, k).astype(jnp.float32) + piece(2 * chip + 1, k).astype(jnp.float32)
    ).astype(jnp.bfloat16)
    queries, keys, values = [], [], []
    for chip in range(n_ctx // 2):
        queries += [piece(2 * chip, 0), piece(2 * chip + 1, 0), both(chip, 3)]
        keys += [piece(2 * chip, 1), piece(2 * chip + 1, 1), both(chip, 4)]
        values += [piece(2 * chip, 2), piece(2 * chip + 1, 2), both(chip, 5)]
    return jnp.concatenate(queries + keys + values, axis=1)


def scan_forward(packed, block_table, seq_length):
    feat_width = HEADS * HEAD_DIM
    tok_rows = packed.shape[0]
    blk_rows = BLK
    score_scale = 1.0 / math.sqrt(HEAD_DIM)
    query_heads = packed[:, :feat_width].reshape(tok_rows, HEADS, HEAD_DIM)
    key_rows = packed[:, feat_width : 2 * feat_width]
    value_rows = packed[:, 2 * feat_width :]
    start_state = (
        jnp.full((HEADS, tok_rows), NEG_FILL, jnp.float32),
        jnp.zeros((HEADS, tok_rows), jnp.float32),
        jnp.zeros((tok_rows, HEADS, HEAD_DIM), jnp.float32),
    )
    key_piece = lax.all_gather(key_rows, "ctx", axis=0, tiled=True)
    value_piece = lax.all_gather(value_rows, "ctx", axis=0, tiled=True)
    piece_rows = key_piece.shape[0]
    fold_blk_size = math.gcd(piece_rows, 1024)
    num_blocks = piece_rows // fold_blk_size
    key_blocks = key_piece.reshape(num_blocks, fold_blk_size, HEADS, HEAD_DIM)
    value_blocks = value_piece.reshape(num_blocks, fold_blk_size, HEADS, HEAD_DIM)
    offsets = fold_blk_size * jnp.arange(num_blocks, dtype=jnp.int32)

    def scan_step(state_in, loop_item):
        running_max, running_sum, accum_out = state_in
        key_blk, value_blk, offset = loop_item
        valid_keys = key_valid(offset, fold_blk_size, blk_rows, block_table, seq_length)
        scores = (
            jnp.einsum("qhd,khd->hqk", query_heads, key_blk, preferred_element_type=jnp.float32)
            * score_scale
        )
        scores = jnp.where(valid_keys[None, None, :], scores, NEG_FILL)
        new_max = jnp.maximum(running_max, jnp.max(scores, axis=2))
        factor = jnp.exp(running_max - new_max)
        soft_weights = jnp.exp(scores - new_max[:, :, None])
        new_sum = running_sum * factor + jnp.sum(soft_weights, axis=2)
        update = jnp.einsum(
            "hqk,khd->qhd",
            soft_weights.astype(jnp.bfloat16),
            value_blk,
            preferred_element_type=jnp.float32,
        )
        accum_out = accum_out * jnp.transpose(factor)[:, :, None] + update
        return ((new_max, new_sum, accum_out), None)

    result, _ = lax.scan(scan_step, start_state, (key_blocks, value_blocks, offsets))
    run_max, run_sum, accum_out = result
    lse = run_max + jnp.log(run_sum)
    attn_heads = accum_out / jnp.transpose(run_sum)[:, :, None]
    context = attn_heads.reshape(tok_rows, feat_width).astype(jnp.bfloat16)
    return context, (query_heads, key_rows, value_rows, lse, attn_heads)


def scan_backward(context_grad, saved, block_table, seq_length):
    query_heads, key_rows, value_rows, lse, attn_heads = saved
    feat_width = HEADS * HEAD_DIM
    tok_rows = context_grad.shape[0]
    blk_rows = BLK
    score_scale = 1.0 / math.sqrt(HEAD_DIM)
    grad_heads = context_grad.reshape(tok_rows, HEADS, HEAD_DIM)
    delta = jnp.einsum("qhd,qhd->hq", grad_heads.astype(jnp.float32), attn_heads)
    gathered_keys, gathered_values = (
        lax.all_gather(key_rows, "ctx", axis=0, tiled=True),
        lax.all_gather(value_rows, "ctx", axis=0, tiled=True),
    )
    total_rows = gathered_keys.shape[0]
    blk_size = math.gcd(total_rows, 1024)
    num_blocks = total_rows // blk_size
    key_blocks = gathered_keys.reshape(num_blocks, blk_size, HEADS, HEAD_DIM)
    value_blocks = gathered_values.reshape(num_blocks, blk_size, HEADS, HEAD_DIM)
    offsets = blk_size * jnp.arange(num_blocks, dtype=jnp.int32)

    def scan_back(query_acc, loop_item):
        key_blk, value_blk, offset = loop_item
        valid_keys = key_valid(offset, blk_size, blk_rows, block_table, seq_length)
        attn_probs = exp_scores(query_heads, key_blk, valid_keys, lse, score_scale)
        value_part = jnp.einsum(
            "hqk,qhd->khd",
            attn_probs.astype(jnp.bfloat16),
            grad_heads,
            preferred_element_type=jnp.float32,
        )
        prob_grad = jnp.einsum(
            "qhd,khd->hqk", grad_heads, value_blk, preferred_element_type=jnp.float32
        )
        score_low = (attn_probs * (prob_grad - delta[:, :, None])).astype(jnp.bfloat16)
        query_acc = (
            query_acc
            + jnp.einsum("hqk,khd->qhd", score_low, key_blk, preferred_element_type=jnp.float32)
            * score_scale
        )
        key_part = (
            jnp.einsum("hqk,qhd->khd", score_low, query_heads, preferred_element_type=jnp.float32)
            * score_scale
        )
        return (
            query_acc,
            jnp.concatenate(
                [key_part.reshape(blk_size, feat_width), value_part.reshape(blk_size, feat_width)],
                axis=1,
            ),
        )

    query_acc, terms = lax.scan(
        scan_back,
        jnp.zeros((tok_rows, HEADS, HEAD_DIM), jnp.float32),
        (key_blocks, value_blocks, offsets),
    )
    key_value_grad = lax.psum_scatter(
        terms.reshape(total_rows, 2 * feat_width), "ctx", scatter_dimension=0, tiled=True
    )
    query_grad = query_acc.reshape(tok_rows, feat_width)
    key_grad = key_value_grad[:, :feat_width]
    value_grad = key_value_grad[:, feat_width:]
    return jnp.concatenate([query_grad, key_grad, value_grad], axis=1).astype(jnp.bfloat16)


def reduce_weight(grad):
    part = lax.psum_scatter(
        grad.astype(jnp.bfloat16), "fsdp", scatter_dimension=0, tiled=True
    ).astype(jnp.float32)
    return lax.psum(part, "ctx")


def local(
    tokens,
    cotangent,
    lengths,
    block_table,
    qkv_weight,
    query_bias,
    value_bias,
    proj_weight,
    proj_bias,
    gain_first,
    shift_first,
    inner_weight,
    inner_bias,
    outer_weight,
    outer_bias,
    gain_second,
    shift_second,
):
    feat_width = HEADS * HEAD_DIM
    tok_rows = tokens.shape[0]
    seq_length = lengths[0]
    n_fsdp = lax.axis_size("fsdp")
    n_ctx = lax.axis_size("ctx")
    dealt = n_ctx == 8 and n_fsdp == 4 and tok_rows == 256
    vectors = (
        query_bias,
        value_bias,
        proj_bias,
        gain_first,
        shift_first,
        inner_bias,
        outer_bias,
        gain_second,
        shift_second,
    )
    ends = [0]
    for vector in vectors:
        ends.append(ends[-1] + vector.shape[0])
    gathered = lax.all_gather(jnp.concatenate(vectors)[None], "fsdp", axis=0, tiled=True)
    (
        qbias_full,
        vbias_full,
        pbias_full,
        gain1_full,
        shift1_full,
        ibias_full,
        obias_full,
        gain2_full,
        shift2_full,
    ) = [gathered[:, ends[k] : ends[k + 1]].reshape(-1) for k in range(len(vectors))]
    if dealt:
        both_full = gather_kernel_call(jnp.concatenate([qkv_weight, proj_weight], axis=1), 5)
        qkv_full = both_full[:, : 3 * feat_width]
        proj_full = both_full[:, 3 * feat_width :]
    else:
        qkv_full, proj_full, inner_full, outer_full = [
            lax.all_gather(weight, "fsdp", axis=0, tiled=True)
            for weight in (qkv_weight, proj_weight, inner_weight, outer_weight)
        ]
    tokens_wide = tokens.astype(jnp.float32)
    bias_row = jnp.concatenate([qbias_full, jnp.zeros_like(qbias_full), vbias_full]).astype(
        jnp.float32
    )
    packed = (jnp.dot(tokens, qkv_full, preferred_element_type=jnp.float32) + bias_row).astype(
        jnp.bfloat16
    )
    if dealt:
        context, saved, inner_full, outer_full = dealt_forward(
            packed, block_table, seq_length, n_ctx, inner_weight, outer_weight
        )
    else:
        context, saved = scan_forward(packed, block_table, seq_length)
    hidden = (
        tokens_wide
        + jnp.dot(context, proj_full, preferred_element_type=jnp.float32)
        + pbias_full.astype(jnp.float32)
    )
    normed, norm_back = jax.vjp(
        layer_norm, hidden, gain1_full.astype(jnp.float32), shift1_full.astype(jnp.float32)
    )
    normed_low = normed.astype(jnp.bfloat16)
    inner_pre = jnp.dot(
        normed_low, inner_full, preferred_element_type=jnp.float32
    ) + ibias_full.astype(jnp.float32)
    active, gelu_back = jax.vjp(gelu_exact, inner_pre)
    active_low = active.astype(jnp.bfloat16)
    mixed_sum = (
        normed
        + jnp.dot(active_low, outer_full, preferred_element_type=jnp.float32)
        + obias_full.astype(jnp.float32)
    )
    result, final_back = jax.vjp(
        layer_norm, mixed_sum, gain2_full.astype(jnp.float32), shift2_full.astype(jnp.float32)
    )
    layer_out = result.astype(jnp.bfloat16)
    mixed_grad, gain2_grad, shift2_grad = final_back(cotangent.astype(jnp.float32))
    branch_low = mixed_grad.astype(jnp.bfloat16)
    outer_grad = cross_dot(active_low, branch_low)
    obias_grad = jnp.sum(branch_low.astype(jnp.float32), axis=0)
    (inner_grad_wide,) = gelu_back(back_dot(branch_low, outer_full))
    inner_low = inner_grad_wide.astype(jnp.bfloat16)
    inner_grad = cross_dot(normed_low, inner_low)
    ibias_grad = jnp.sum(inner_low.astype(jnp.float32), axis=0)
    normed_grad = mixed_grad + back_dot(inner_low, inner_full)
    hidden_grad, gain1_grad, shift1_grad = norm_back(normed_grad)
    proj_low = hidden_grad.astype(jnp.bfloat16)
    proj_grad = cross_dot(context, proj_low)
    pbias_grad = jnp.sum(proj_low.astype(jnp.float32), axis=0)
    context_grad = back_dot(proj_low, proj_full).astype(jnp.bfloat16)
    if dealt:
        packed_grad = dealt_backward(context_grad, saved, n_ctx)
    else:
        packed_grad = scan_backward(context_grad, saved, block_table, seq_length)
    qkv_grad = cross_dot(tokens, packed_grad)
    qbias_grad = jnp.sum(packed_grad[:, :feat_width].astype(jnp.float32), axis=0)
    vbias_grad = jnp.sum(packed_grad[:, 2 * feat_width :].astype(jnp.float32), axis=0)
    tokens_grad = (hidden_grad + back_dot(packed_grad, qkv_full)).astype(jnp.bfloat16)
    sums = (
        qbias_grad,
        vbias_grad,
        pbias_grad,
        gain1_grad,
        shift1_grad,
        ibias_grad,
        obias_grad,
        gain2_grad,
        shift2_grad,
    )
    bundle = jnp.concatenate([total.reshape(n_fsdp, -1) for total in sums], axis=1)
    bundle = lax.psum(bundle, ("fsdp", "ctx"))
    bundle = lax.dynamic_index_in_dim(bundle, lax.axis_index("fsdp"), axis=0, keepdims=False)
    vector_parts = [bundle[ends[k] : ends[k + 1]] for k in range(len(sums))]
    if dealt:
        low = jnp.bfloat16
        inner_sum, outer_sum, attn_sum = reduce_grads(
            [
                split_wide(inner_grad.astype(low)),
                outer_grad.astype(low).reshape(4, feat_width, feat_width),
                jnp.concatenate(
                    [
                        split_wide(qkv_grad.astype(low)),
                        proj_grad.astype(low).reshape(4, feat_width // 4, feat_width),
                    ],
                    axis=1,
                ),
            ]
        )
        shard_rows = feat_width // 4
        inner_sum = join_wide(inner_sum, shard_rows)
        qkv_sum = join_wide(attn_sum[: 3 * shard_rows], shard_rows)
        proj_sum = attn_sum[3 * shard_rows :]
    else:
        qkv_sum, proj_sum, inner_sum, outer_sum = [
            reduce_weight(grad) for grad in (qkv_grad, proj_grad, inner_grad, outer_grad)
        ]
    return (
        layer_out,
        tokens_grad,
        qkv_sum,
        vector_parts[0],
        vector_parts[1],
        proj_sum,
        vector_parts[2],
        vector_parts[3],
        vector_parts[4],
        inner_sum,
        vector_parts[5],
        outer_sum,
        vector_parts[6],
        vector_parts[7],
        vector_parts[8],
    )


def solution(mesh):
    placed = (
        P(("fsdp", "ctx"), None),
        P(("fsdp", "ctx"), None),
        P("fsdp"),
        P(),
        P("fsdp", None),
        P("fsdp"),
        P("fsdp"),
        P("fsdp", None),
        P("fsdp"),
        P("fsdp"),
        P("fsdp"),
        P("fsdp", None),
        P("fsdp"),
        P("fsdp", None),
        P("fsdp"),
        P("fsdp"),
        P("fsdp"),
    )
    return jax.shard_map(
        local,
        mesh=mesh,
        in_specs=placed,
        out_specs=(
            P(("fsdp", "ctx"), None),
            P(("fsdp", "ctx"), None),
            P("fsdp", None),
            P("fsdp"),
            P("fsdp"),
            P("fsdp", None),
            P("fsdp"),
            P("fsdp"),
            P("fsdp"),
            P("fsdp", None),
            P("fsdp"),
            P("fsdp", None),
            P("fsdp"),
            P("fsdp"),
            P("fsdp"),
        ),
        check_vma=False,
    )
```

```python
import functools
import math

import jax
import jax.numpy as jnp
from jax import lax
from jax.experimental import pallas as pl
from jax.experimental.pallas import tpu as pltpu
from jax.sharding import PartitionSpec as P

HEADS = 12
HEAD_DIM = 64
BLK = 128


NEG_FILL = -1e30
NORM_EPS = 1e-05


def layer_norm(vector_in, gain_in, shift_in):
    center = vector_in - jnp.mean(vector_in, axis=-1, keepdims=True)
    spread = jnp.mean(center * center, axis=-1, keepdims=True)
    return center * lax.rsqrt(spread + NORM_EPS) * gain_in + shift_in


def gelu_exact(vector_in):
    return jax.nn.gelu(vector_in, approximate=False)


def cross_dot(first_op, second_op):
    return lax.dot_general(
        first_op, second_op, (((0,), (0,)), ((), ())), preferred_element_type=jnp.float32
    )


def back_dot(first_op, second_op):
    return lax.dot_general(
        first_op, second_op, (((1,), (1,)), ((), ())), preferred_element_type=jnp.float32
    )


def key_valid(start_row, piece_rows, blk_rows, block_table, seq_length):
    index_rows = start_row + jnp.arange(piece_rows, dtype=jnp.int32)
    owner_block = index_rows // blk_rows
    table_slots = jnp.arange(block_table.shape[0], dtype=jnp.int32)
    placed = jnp.sum(
        jnp.where(owner_block[:, None] == table_slots[None, :], block_table[None, :], 0), axis=1
    )
    return placed * blk_rows + index_rows % blk_rows < seq_length


def exp_scores(query_blk, key_blk, valid_keys, lse_blk, score_scale):
    scores = (
        jnp.einsum("qhd,khd->hqk", query_blk, key_blk, preferred_element_type=jnp.float32)
        * score_scale
    )
    scores = jnp.where(valid_keys[None, None, :], scores, NEG_FILL)
    return jnp.exp(scores - lse_blk[:, :, None])


MESH_IDS = pl.DeviceIdType.MESH


def beside():
    f = lax.axis_index("fsdp")
    c = lax.axis_index("ctx")
    x, y = lax.rem(f, 2), f // 2
    core = lax.rem(c, 2)
    over_x = 2 * y + (1 - x)
    over_y = 2 * (1 - y) + x
    over_both = 2 * (1 - y) + (1 - x)
    return f, over_x, over_y, over_both, core, c + 1 - 2 * core


def greet(targets):
    barrier = pltpu.get_barrier_semaphore()
    for target in targets:
        pl.semaphore_signal(barrier, inc=1, device_id=target, device_id_type=MESH_IDS)
    pl.semaphore_wait(barrier, len(targets))


def remote(source, target, send, recv, device):
    return pltpu.make_async_remote_copy(
        src_ref=source,
        dst_ref=target,
        send_sem=send,
        recv_sem=recv,
        device_id=device,
        device_id_type=MESH_IDS,
    )


class Swap:
    def __init__(self, n, x_ref, y_ref, send_sem, recv_sem, own_sem):
        self.n, self.x_ref, self.y_ref = n, x_ref, y_ref
        self.send_sem, self.recv_sem, self.own_sem = send_sem, recv_sem, own_sem
        self.me = lax.axis_index("ctx")
        self.own = pltpu.make_async_copy(x_ref.at[self.me], y_ref.at[self.me], own_sem)

    def targets(self):
        return [{"ctx": lax.rem(self.me + step, self.n)} for step in range(1, self.n)]

    def start(self):
        self.own.start()
        for step in range(1, self.n):
            peer = lax.rem(self.me + step, self.n)
            remote(
                self.x_ref.at[peer],
                self.y_ref.at[self.me],
                self.send_sem.at[step],
                self.recv_sem.at[step],
                {"ctx": peer},
            ).start()

    def finish(self):
        self.own.wait()
        for step in range(1, self.n):
            source = lax.rem(self.me + self.n - step, self.n)
            remote(
                self.x_ref.at[source],
                self.y_ref.at[source],
                self.send_sem.at[step],
                self.recv_sem.at[step],
                {"ctx": source},
            ).wait()


class Gather:
    def __init__(self, w_ref, o_ref, send_sem, recv_sem, own_sem):
        self.w_ref, self.o_ref = w_ref, o_ref
        self.f, self.fx, self.fy, self.fd, self.core, self.sibling = beside()
        half = w_ref.shape[1] // 2
        upper, lower = pl.ds(0, half), pl.ds(half, half)
        f, fx, fy, fd, k = self.f, self.fx, self.fy, self.fd, self.core
        to_x, to_y, to_core = {"fsdp": fx}, {"fsdp": fy}, {"ctx": self.sibling}
        o = o_ref

        def copy(number, source, target, device):
            return remote(source, target, send_sem.at[number], recv_sem.at[number], device)

        self.own = pltpu.make_async_copy(w_ref, o.at[f], own_sem)
        self.sends = [
            copy(0, w_ref.at[k], o.at[f, k], to_x),
            copy(1, w_ref.at[k], o.at[f, k], to_y),
            copy(2, o.at[fx, k, upper], o.at[fx, k, upper], to_y),
            copy(3, o.at[fx, k], o.at[fx, k], to_core),
            copy(4, o.at[fy, k, lower], o.at[fy, k, lower], to_x),
            copy(5, o.at[fy, k], o.at[fy, k], to_core),
            copy(6, o.at[fd, k], o.at[fd, k], to_core),
        ]
        other = 1 - k
        self.takes = [
            copy(0, w_ref.at[k], o.at[fx, k], to_x),
            copy(1, w_ref.at[k], o.at[fy, k], to_y),
            copy(2, o.at[fd, k, upper], o.at[fd, k, upper], to_y),
            copy(3, o.at[fx, other], o.at[fx, other], to_core),
            copy(4, o.at[fd, k, lower], o.at[fd, k, lower], to_x),
            copy(5, o.at[fy, other], o.at[fy, other], to_core),
            copy(6, o.at[fd, other], o.at[fd, other], to_core),
        ]

    def targets(self):
        return [{"fsdp": self.fx}, {"fsdp": self.fy}]

    def start(self):
        self.sends[0].start()
        self.sends[1].start()
        self.own.start()

    def finish(self):
        self.takes[0].wait_recv()
        self.sends[2].start()
        self.sends[3].start()
        self.takes[1].wait_recv()
        self.sends[4].start()
        self.sends[5].start()
        self.takes[2].wait_recv()
        self.takes[4].wait_recv()
        self.sends[6].start()
        for number in (3, 5, 6):
            self.takes[number].wait_recv()
        self.own.wait()
        for send in self.sends:
            send.wait_send()


def swap_kernel(n, x_ref, y_ref, *sems):
    swap = Swap(n, x_ref, y_ref, *sems)
    greet(swap.targets())
    swap.start()
    swap.finish()


def gather_kernel(w_ref, o_ref, *sems):
    gather = Gather(w_ref, o_ref, *sems)
    greet(gather.targets() + [{"ctx": gather.sibling}])
    gather.start()
    gather.finish()


def swap_gather_kernel(n, x_ref, w_ref, y_ref, o_ref, *sems):
    swap = Swap(n, x_ref, y_ref, *sems[:3])
    gather = Gather(w_ref, o_ref, *sems[3:])
    greet(swap.targets() + gather.targets())
    gather.start()
    swap.start()
    gather.finish()
    swap.finish()


def vmem_specs(count):
    return [pl.BlockSpec(memory_space=pltpu.VMEM)] * count


def copy_sems(count):
    return [
        pltpu.SemaphoreType.DMA((count,)),
        pltpu.SemaphoreType.DMA((count,)),
        pltpu.SemaphoreType.DMA,
    ]


def linked(number, limit):
    return pltpu.CompilerParams(
        collective_id=number, has_side_effects=True, vmem_limit_bytes=limit << 20
    )


def exchange(blocks, number):
    n = blocks.shape[0]
    return pl.pallas_call(
        functools.partial(swap_kernel, n),
        out_shape=jax.ShapeDtypeStruct(blocks.shape, blocks.dtype),
        in_specs=vmem_specs(1),
        out_specs=vmem_specs(1)[0],
        scratch_shapes=copy_sems(n),
        compiler_params=linked(number, 16),
    )(blocks)


def gather_kernel_call(shard, number):
    rows, columns = shard.shape
    whole = pl.pallas_call(
        gather_kernel,
        out_shape=jax.ShapeDtypeStruct((4, 2, rows // 2, columns), shard.dtype),
        in_specs=vmem_specs(1),
        out_specs=vmem_specs(1)[0],
        scratch_shapes=copy_sems(7),
        compiler_params=linked(number, 16),
    )(shard.reshape(2, rows // 2, columns))
    return whole.reshape(4 * rows, columns)


def exchange_gather(blocks, shard, number):
    n = blocks.shape[0]
    rows, columns = shard.shape
    swapped, whole = pl.pallas_call(
        functools.partial(swap_gather_kernel, n),
        out_shape=[
            jax.ShapeDtypeStruct(blocks.shape, blocks.dtype),
            jax.ShapeDtypeStruct((4, 2, rows // 2, columns), shard.dtype),
        ],
        in_specs=vmem_specs(2),
        out_specs=vmem_specs(2),
        scratch_shapes=copy_sems(n) + copy_sems(7),
        compiler_params=linked(number, 24),
    )(blocks, shard.reshape(2, rows // 2, columns))
    return swapped, whole.reshape(4 * rows, columns)


CHUNKS = 3


def wide_sum(*parts):
    total = parts[0].astype(jnp.float32)
    for part in parts[1:]:
        total = total + part.astype(jnp.float32)
    return total.astype(jnp.bfloat16)


def reduce_kernel(*refs):
    ins, outs = refs[:CHUNKS], refs[CHUNKS : 2 * CHUNKS]
    halves, side, turn, deep, send_sem, recv_sem = refs[2 * CHUNKS :]
    f, fx, fy, _, k, sibling = beside()
    c = lax.axis_index("ctx")
    z = c // 2
    x, y = lax.rem(f, 2), f // 2
    to_x, to_y, to_core = {"fsdp": fx}, {"fsdp": fy}, {"ctx": sibling}
    depth = [lax.rem(z + step, 4) for step in range(1, 4)]
    source = [lax.rem(z + 4 - step, 4) for step in range(1, 4)]
    to_z = [{"ctx": 2 * peer + k} for peer in depth]
    low, high = pl.ds(0, 2), pl.ds(2, 2)

    def copy(j, number, origin, target, device):
        return remote(origin, target, send_sem.at[j, number], recv_sem.at[j, number], device)

    def core_copies(j):
        return [
            copy(j, g, ins[j].at[g, 1 - k], halves.at[j, g], to_core) for g in range(4)
        ]

    def side_copies(j):
        copies = []
        for t in range(2):
            goes = 2 * t + (1 - x)
            copies.append(copy(j, 4 + t, halves.at[j, goes, low], side.at[j, t], to_x))
            goes = 2 * (1 - y) + t
            copies.append(copy(j, 6 + t, halves.at[j, goes, high], side.at[j, 2 + t], to_y))
        return copies

    def turn_copies(j):
        return [
            copy(j, 8, halves.at[j, fy, low], turn.at[j, 0], to_y),
            copy(j, 9, halves.at[j, fx, high], turn.at[j, 1], to_x),
        ]

    def deep_copies(j):
        return [
            copy(j, 10 + i, halves.at[j, f, depth[i]], deep.at[j, i], to_z[i]) for i in range(3)
        ]

    def back_copies(j):
        return [copy(j, 13 + i, outs[j].at[k, z], outs[j].at[k, z], to_z[i]) for i in range(3)]

    def back_takes(j):
        return [
            copy(j, 13 + i, outs[j].at[k, source[i]], outs[j].at[k, source[i]], to_z[i])
            for i in range(3)
        ]

    def last_copy(j):
        return copy(j, 16, outs[j].at[k], outs[j].at[k], to_core)

    def last_take(j):
        return copy(j, 16, outs[j].at[1 - k], outs[j].at[1 - k], to_core)

    def start_all(copies):
        for one in copies:
            one.start()

    def take_all(copies):
        for one in copies:
            one.wait_recv()

    def phase_core(j):
        take_all(core_copies(j))

        @pl.loop(0, 16)
        def _(i):
            g, d = i // 4, lax.rem(i, 4)
            halves[j, g, d] = wide_sum(halves[j, g, d], ins[j][g, k, d])

        start_all(side_copies(j))

    def phase_side(j):
        copies = side_copies(j)
        for one in copies:
            one.wait()

        @pl.loop(0, 2)
        def _(d):
            for t in range(2):
                keeps = 2 * t + x
                halves[j, keeps, d] = wide_sum(halves[j, keeps, d], side[j, t, d])
                keeps = 2 * y + t
                halves[j, keeps, 2 + d] = wide_sum(halves[j, keeps, 2 + d], side[j, 2 + t, d])

        start_all(turn_copies(j))

    def phase_turn(j):
        for one in turn_copies(j):
            one.wait()

        @pl.loop(0, 2)
        def _(d):
            halves[j, f, d] = wide_sum(halves[j, f, d], turn[j, 0, d])
            halves[j, f, 2 + d] = wide_sum(halves[j, f, 2 + d], turn[j, 1, d])

        start_all(deep_copies(j))

    def phase_deep(j):
        take_all(deep_copies(j))
        outs[j][k, z] = wide_sum(halves[j, f, z], deep[j, 0], deep[j, 1], deep[j, 2])
        start_all(back_copies(j))

    def phase_back(j):
        take_all(back_takes(j))
        last_copy(j).start()

    def phase_last(j):
        last_take(j).wait_recv()
        for one in core_copies(j) + deep_copies(j) + back_copies(j) + [last_copy(j)]:
            one.wait_send()

    greet([to_x, to_y, to_core] + to_z)
    for j in range(CHUNKS):
        start_all(core_copies(j))
    phases = [phase_core, phase_side, phase_turn, phase_deep, phase_back, phase_last]
    for tick in range(CHUNKS + len(phases) - 1):
        for order in reversed(range(len(phases))):
            if 0 <= tick - order < CHUNKS:
                phases[order](tick - order)


def reduce_grads(chunks):
    count, rows, width = chunks[0].shape
    piece = rows // 8
    shaped = [chunk.reshape(4, 2, 4, piece, width) for chunk in chunks]
    low = jnp.bfloat16
    outs = pl.pallas_call(
        reduce_kernel,
        out_shape=[jax.ShapeDtypeStruct((2, 4, piece, width), low)] * CHUNKS,
        in_specs=vmem_specs(CHUNKS),
        out_specs=vmem_specs(CHUNKS),
        scratch_shapes=[
            pltpu.VMEM((CHUNKS, 4, 4, piece, width), low),
            pltpu.VMEM((CHUNKS, 4, 2, piece, width), low),
            pltpu.VMEM((CHUNKS, 2, 2, piece, width), low),
            pltpu.VMEM((CHUNKS, 3, piece, width), low),
            pltpu.SemaphoreType.DMA((CHUNKS, 17)),
            pltpu.SemaphoreType.DMA((CHUNKS, 17)),
        ],
        compiler_params=linked(6, 48),
    )(*shaped)
    return [out.reshape(rows, width).astype(jnp.float32) for out in outs]


def split_wide(grad):
    rows, columns = grad.shape
    feat_width = HEADS * HEAD_DIM
    shards = grad.reshape(4, rows // 4, columns)
    return jnp.concatenate(
        [shards[:, :, at : at + feat_width] for at in range(0, columns, feat_width)], axis=1
    )


def join_wide(shard, rows):
    return jnp.concatenate(
        [shard[at : at + rows] for at in range(0, shard.shape[0], rows)], axis=1
    )


def bundle_kernel(n, x_ref, o_ref, near, far, send_sem, recv_sem):
    f, c = lax.axis_index("fsdp"), lax.axis_index("ctx")
    near_to = [lax.rem(f + step, 4) for step in range(1, 4)]
    far_to = [{"ctx": lax.rem(c + step, n)} for step in range(1, n)]
    greet([{"fsdp": peer} for peer in near_to] + far_to)
    first = [
        remote(x_ref.at[near_to[i]], near.at[i], send_sem.at[i], recv_sem.at[i], {"fsdp": near_to[i]})
        for i in range(3)
    ]
    for one in first:
        one.start()
    for one in first:
        one.wait()
    far[c] = x_ref[f] + near[0] + near[1] + near[2]
    for i in range(n - 1):
        remote(
            far.at[c], far.at[c], send_sem.at[3 + i], recv_sem.at[3 + i], far_to[i]
        ).start()
    for i in range(n - 1):
        source = lax.rem(c + n - 1 - i, n)
        remote(
            far.at[source], far.at[source], send_sem.at[3 + i], recv_sem.at[3 + i], far_to[i]
        ).wait()
    total = far[0]
    for i in range(1, n):
        total = total + far[i]
    o_ref[...] = total


def reduce_bundle(bundle, n):
    width = bundle.shape[1]
    rows = -(-width // 1024) * 8
    padded = jnp.pad(bundle, ((0, 0), (0, rows * 128 - width))).reshape(4, rows, 128)
    total = pl.pallas_call(
        functools.partial(bundle_kernel, n),
        out_shape=jax.ShapeDtypeStruct((rows, 128), jnp.float32),
        in_specs=vmem_specs(1),
        out_specs=vmem_specs(1)[0],
        scratch_shapes=[
            pltpu.VMEM((3, rows, 128), jnp.float32),
            pltpu.VMEM((n, rows, 128), jnp.float32),
            pltpu.SemaphoreType.DMA((n + 2,)),
            pltpu.SemaphoreType.DMA((n + 2,)),
        ],
        compiler_params=linked(7, 8),
    )(padded)
    return total.reshape(-1)[:width]


QTILE = 512


def attend_kernel(query_ref, key_ref, value_ref, out_ref, lse_ref):
    scores = lax.dot_general(
        key_ref[0], query_ref[...], (((1,), (1,)), ((), ())), preferred_element_type=jnp.float32
    )
    top = jnp.max(scores, axis=0, keepdims=True)
    weights = jnp.exp(scores - top)
    total = jnp.sum(weights, axis=0, keepdims=True)
    out = jnp.dot(value_ref[0], weights.astype(jnp.bfloat16), preferred_element_type=jnp.float32)
    out_ref[...] = out / total
    lse_ref[...] = top + jnp.log(total)


def attend(query, key, value_t):
    rows, keys = query.shape[0], key.shape[1]
    tiles_first = keys // QTILE
    return pl.pallas_call(
        attend_kernel,
        grid=(rows // QTILE,),
        in_specs=[
            pl.BlockSpec((QTILE, 2 * HEAD_DIM), lambda i: (i, 0)),
            pl.BlockSpec((1, keys, 2 * HEAD_DIM), lambda i: (i // tiles_first, 0, 0)),
            pl.BlockSpec((1, HEAD_DIM, keys), lambda i: (i // tiles_first, 0, 0)),
        ],
        out_specs=[
            pl.BlockSpec((HEAD_DIM, QTILE), lambda i: (0, i)),
            pl.BlockSpec((1, QTILE), lambda i: (0, i)),
        ],
        out_shape=[
            jax.ShapeDtypeStruct((HEAD_DIM, rows), jnp.float32),
            jax.ShapeDtypeStruct((1, rows), jnp.float32),
        ],
        compiler_params=pltpu.CompilerParams(vmem_limit_bytes=40 << 20),
        cost_estimate=pl.CostEstimate(
            flops=4 * rows * keys * HEAD_DIM, bytes_accessed=8 << 20, transcendentals=rows * keys
        ),
    )(query, key, value_t)


def attend_back_kernel(
    tiles_first,
    query_ref,
    key_ref,
    key_t_ref,
    value_ref,
    grad_ref,
    out_ref,
    grad_t_ref,
    lse_ref,
    dquery_ref,
    dkey_ref,
    dvalue_ref,
):
    step = pl.program_id(0)
    scores = back_dot(key_ref[0], query_ref[...])
    probs = jnp.exp(scores - lse_ref[...])
    delta = jnp.sum(out_ref[...] * grad_t_ref[...].astype(jnp.float32), axis=0, keepdims=True)
    prob_grad = back_dot(value_ref[0], grad_ref[...])
    score_low = (probs * (prob_grad - delta)).astype(jnp.bfloat16)
    dquery_ref[...] = jnp.dot(key_t_ref[0], score_low, preferred_element_type=jnp.float32)
    dkey = jnp.dot(score_low, query_ref[...], preferred_element_type=jnp.float32)
    dvalue = jnp.dot(
        probs.astype(jnp.bfloat16), grad_ref[...], preferred_element_type=jnp.float32
    )
    first = lax.rem(step, tiles_first) == 0

    @pl.when(first)
    def _():
        dkey_ref[0] = dkey
        dvalue_ref[0] = dvalue

    @pl.when(jnp.logical_not(first))
    def _():
        dkey_ref[0] += dkey
        dvalue_ref[0] += dvalue


def attend_back(query, key, key_t, value, grad, out, grad_t, lse):
    rows, keys = query.shape[0], key.shape[1]
    tiles_first = keys // QTILE
    pair = lambda i: (i // tiles_first, 0, 0)
    return pl.pallas_call(
        functools.partial(attend_back_kernel, tiles_first),
        grid=(rows // QTILE,),
        in_specs=[
            pl.BlockSpec((QTILE, 2 * HEAD_DIM), lambda i: (i, 0)),
            pl.BlockSpec((1, keys, 2 * HEAD_DIM), pair),
            pl.BlockSpec((1, HEAD_DIM, keys), pair),
            pl.BlockSpec((1, keys, HEAD_DIM), pair),
            pl.BlockSpec((QTILE, HEAD_DIM), lambda i: (i, 0)),
            pl.BlockSpec((HEAD_DIM, QTILE), lambda i: (0, i)),
            pl.BlockSpec((HEAD_DIM, QTILE), lambda i: (0, i)),
            pl.BlockSpec((1, QTILE), lambda i: (0, i)),
        ],
        out_specs=[
            pl.BlockSpec((HEAD_DIM, QTILE), lambda i: (0, i)),
            pl.BlockSpec((1, keys, 2 * HEAD_DIM), pair),
            pl.BlockSpec((1, keys, HEAD_DIM), pair),
        ],
        out_shape=[
            jax.ShapeDtypeStruct((HEAD_DIM, rows), jnp.float32),
            jax.ShapeDtypeStruct((2, keys, 2 * HEAD_DIM), jnp.float32),
            jax.ShapeDtypeStruct((2, keys, HEAD_DIM), jnp.float32),
        ],
        compiler_params=pltpu.CompilerParams(vmem_limit_bytes=52 << 20),
        cost_estimate=pl.CostEstimate(
            flops=10 * rows * keys * HEAD_DIM, bytes_accessed=12 << 20, transcendentals=rows * keys
        ),
    )(query, key, key_t, value, grad, out, grad_t, lse)


def pick_heads(columns, heads):
    return jnp.concatenate([columns[:, h * HEAD_DIM : (h + 1) * HEAD_DIM] for h in heads], axis=1)


def unit_heads(target):
    return 3 * (target // 2) + target % 2, 3 * (target // 2) + 2


def dealt_forward(packed, block_table, seq_length, n_ctx, inner_weight, outer_weight):
    rows = packed.shape[0]
    half = n_ctx // 2 * rows
    core = lax.axis_index("ctx") % 2
    sends = []
    for target in range(n_ctx):
        whole, shared = unit_heads(target)
        sends.append(
            pick_heads(
                packed,
                [whole, HEADS + whole, 2 * HEADS + whole, shared, HEADS + shared, 2 * HEADS + shared],
            )
        )
    got, inner_full = exchange_gather(jnp.stack(sends), inner_weight, 1)
    got = got.reshape(n_ctx * rows, 6, HEAD_DIM)
    total = n_ctx * rows
    valid = key_valid(0, total, BLK, block_table, seq_length)
    mask_col = jnp.where(valid, 0.0, NEG_FILL).astype(jnp.bfloat16)[:, None]
    query = jnp.concatenate(
        [got[:, 0], lax.dynamic_slice_in_dim(got[:, 3], core * half, half, axis=0)], axis=0
    ) * jnp.bfloat16(1.0 / math.sqrt(HEAD_DIM))
    ones_col = jnp.ones((query.shape[0], 1), jnp.bfloat16)
    query = jnp.concatenate(
        [query, ones_col, jnp.zeros((query.shape[0], HEAD_DIM - 1), jnp.bfloat16)], axis=1
    )
    fill = jnp.zeros((total, HEAD_DIM - 1), jnp.bfloat16)
    key = jnp.stack(
        [
            jnp.concatenate([got[:, 1], mask_col, fill], axis=1),
            jnp.concatenate([got[:, 4], mask_col, fill], axis=1),
        ]
    )
    value = jnp.stack([got[:, 2], got[:, 5]])
    out, lse = attend(query, key, jnp.swapaxes(value, 1, 2))
    low = jnp.transpose(out.astype(jnp.bfloat16))
    first = low[:total].reshape(n_ctx, rows, HEAD_DIM)
    second = lax.dynamic_update_slice_in_dim(
        jnp.zeros((total, HEAD_DIM), jnp.bfloat16), low[total:], core * half, axis=0
    ).reshape(n_ctx, rows, HEAD_DIM)
    back, outer_full = exchange_gather(
        jnp.concatenate([first, second], axis=2), outer_weight, 2
    )
    upper = lax.axis_index("ctx") >= n_ctx // 2
    pieces = []
    for chip in range(n_ctx // 2):
        pieces += [
            back[2 * chip, :, :HEAD_DIM],
            back[2 * chip + 1, :, :HEAD_DIM],
            jnp.where(upper, back[2 * chip + 1, :, HEAD_DIM:], back[2 * chip, :, HEAD_DIM:]),
        ]
    context = jnp.concatenate(pieces, axis=1)
    return context, (query, key, value, out, lse), inner_full, outer_full


def dealt_backward(context_grad, saved, n_ctx):
    query, key, value, out, lse = saved
    rows = context_grad.shape[0]
    total = n_ctx * rows
    half = total // 2
    core = lax.axis_index("ctx") % 2
    sends = jnp.stack([pick_heads(context_grad, unit_heads(target)) for target in range(n_ctx)])
    got = exchange(sends, 3).reshape(total, 2 * HEAD_DIM)
    grad = jnp.concatenate(
        [
            got[:, :HEAD_DIM],
            lax.dynamic_slice_in_dim(got[:, HEAD_DIM:], core * half, half, axis=0),
        ],
        axis=0,
    )
    key_t = jnp.swapaxes(key[:, :, :HEAD_DIM], 1, 2)
    dquery_t, dkey, dvalue = attend_back(
        query, key, key_t, value, grad, out, jnp.transpose(grad), lse
    )
    dquery = jnp.transpose((dquery_t * (1.0 / math.sqrt(HEAD_DIM))).astype(jnp.bfloat16))
    dkey = dkey[:, :, :HEAD_DIM].astype(jnp.bfloat16)
    dvalue = dvalue.astype(jnp.bfloat16)
    dshared = lax.dynamic_update_slice_in_dim(
        jnp.zeros((total, HEAD_DIM), jnp.bfloat16), dquery[total:], core * half, axis=0
    )
    sends = jnp.concatenate(
        [dquery[:total], dkey[0], dvalue[0], dshared, dkey[1], dvalue[1]], axis=1
    ).reshape(n_ctx, rows, 6 * HEAD_DIM)
    back = exchange(sends, 4)
    piece = lambda source, k: back[source, :, k * HEAD_DIM : (k + 1) * HEAD_DIM]
    both = lambda chip, k: (
        piece(2 * chip, k).astype(jnp.float32) + piece(2 * chip + 1, k).astype(jnp.float32)
    ).astype(jnp.bfloat16)
    queries, keys, values = [], [], []
    for chip in range(n_ctx // 2):
        queries += [piece(2 * chip, 0), piece(2 * chip + 1, 0), both(chip, 3)]
        keys += [piece(2 * chip, 1), piece(2 * chip + 1, 1), both(chip, 4)]
        values += [piece(2 * chip, 2), piece(2 * chip + 1, 2), both(chip, 5)]
    return jnp.concatenate(queries + keys + values, axis=1)


def scan_forward(packed, block_table, seq_length):
    feat_width = HEADS * HEAD_DIM
    tok_rows = packed.shape[0]
    blk_rows = BLK
    score_scale = 1.0 / math.sqrt(HEAD_DIM)
    query_heads = packed[:, :feat_width].reshape(tok_rows, HEADS, HEAD_DIM)
    key_rows = packed[:, feat_width : 2 * feat_width]
    value_rows = packed[:, 2 * feat_width :]
    start_state = (
        jnp.full((HEADS, tok_rows), NEG_FILL, jnp.float32),
        jnp.zeros((HEADS, tok_rows), jnp.float32),
        jnp.zeros((tok_rows, HEADS, HEAD_DIM), jnp.float32),
    )
    key_piece = lax.all_gather(key_rows, "ctx", axis=0, tiled=True)
    value_piece = lax.all_gather(value_rows, "ctx", axis=0, tiled=True)
    piece_rows = key_piece.shape[0]
    fold_blk_size = math.gcd(piece_rows, 1024)
    num_blocks = piece_rows // fold_blk_size
    key_blocks = key_piece.reshape(num_blocks, fold_blk_size, HEADS, HEAD_DIM)
    value_blocks = value_piece.reshape(num_blocks, fold_blk_size, HEADS, HEAD_DIM)
    offsets = fold_blk_size * jnp.arange(num_blocks, dtype=jnp.int32)

    def scan_step(state_in, loop_item):
        running_max, running_sum, accum_out = state_in
        key_blk, value_blk, offset = loop_item
        valid_keys = key_valid(offset, fold_blk_size, blk_rows, block_table, seq_length)
        scores = (
            jnp.einsum("qhd,khd->hqk", query_heads, key_blk, preferred_element_type=jnp.float32)
            * score_scale
        )
        scores = jnp.where(valid_keys[None, None, :], scores, NEG_FILL)
        new_max = jnp.maximum(running_max, jnp.max(scores, axis=2))
        factor = jnp.exp(running_max - new_max)
        soft_weights = jnp.exp(scores - new_max[:, :, None])
        new_sum = running_sum * factor + jnp.sum(soft_weights, axis=2)
        update = jnp.einsum(
            "hqk,khd->qhd",
            soft_weights.astype(jnp.bfloat16),
            value_blk,
            preferred_element_type=jnp.float32,
        )
        accum_out = accum_out * jnp.transpose(factor)[:, :, None] + update
        return ((new_max, new_sum, accum_out), None)

    result, _ = lax.scan(scan_step, start_state, (key_blocks, value_blocks, offsets))
    run_max, run_sum, accum_out = result
    lse = run_max + jnp.log(run_sum)
    attn_heads = accum_out / jnp.transpose(run_sum)[:, :, None]
    context = attn_heads.reshape(tok_rows, feat_width).astype(jnp.bfloat16)
    return context, (query_heads, key_rows, value_rows, lse, attn_heads)


def scan_backward(context_grad, saved, block_table, seq_length):
    query_heads, key_rows, value_rows, lse, attn_heads = saved
    feat_width = HEADS * HEAD_DIM
    tok_rows = context_grad.shape[0]
    blk_rows = BLK
    score_scale = 1.0 / math.sqrt(HEAD_DIM)
    grad_heads = context_grad.reshape(tok_rows, HEADS, HEAD_DIM)
    delta = jnp.einsum("qhd,qhd->hq", grad_heads.astype(jnp.float32), attn_heads)
    gathered_keys, gathered_values = (
        lax.all_gather(key_rows, "ctx", axis=0, tiled=True),
        lax.all_gather(value_rows, "ctx", axis=0, tiled=True),
    )
    total_rows = gathered_keys.shape[0]
    blk_size = math.gcd(total_rows, 1024)
    num_blocks = total_rows // blk_size
    key_blocks = gathered_keys.reshape(num_blocks, blk_size, HEADS, HEAD_DIM)
    value_blocks = gathered_values.reshape(num_blocks, blk_size, HEADS, HEAD_DIM)
    offsets = blk_size * jnp.arange(num_blocks, dtype=jnp.int32)

    def scan_back(query_acc, loop_item):
        key_blk, value_blk, offset = loop_item
        valid_keys = key_valid(offset, blk_size, blk_rows, block_table, seq_length)
        attn_probs = exp_scores(query_heads, key_blk, valid_keys, lse, score_scale)
        value_part = jnp.einsum(
            "hqk,qhd->khd",
            attn_probs.astype(jnp.bfloat16),
            grad_heads,
            preferred_element_type=jnp.float32,
        )
        prob_grad = jnp.einsum(
            "qhd,khd->hqk", grad_heads, value_blk, preferred_element_type=jnp.float32
        )
        score_low = (attn_probs * (prob_grad - delta[:, :, None])).astype(jnp.bfloat16)
        query_acc = (
            query_acc
            + jnp.einsum("hqk,khd->qhd", score_low, key_blk, preferred_element_type=jnp.float32)
            * score_scale
        )
        key_part = (
            jnp.einsum("hqk,qhd->khd", score_low, query_heads, preferred_element_type=jnp.float32)
            * score_scale
        )
        return (
            query_acc,
            jnp.concatenate(
                [key_part.reshape(blk_size, feat_width), value_part.reshape(blk_size, feat_width)],
                axis=1,
            ),
        )

    query_acc, terms = lax.scan(
        scan_back,
        jnp.zeros((tok_rows, HEADS, HEAD_DIM), jnp.float32),
        (key_blocks, value_blocks, offsets),
    )
    key_value_grad = lax.psum_scatter(
        terms.reshape(total_rows, 2 * feat_width), "ctx", scatter_dimension=0, tiled=True
    )
    query_grad = query_acc.reshape(tok_rows, feat_width)
    key_grad = key_value_grad[:, :feat_width]
    value_grad = key_value_grad[:, feat_width:]
    return jnp.concatenate([query_grad, key_grad, value_grad], axis=1).astype(jnp.bfloat16)


def reduce_weight(grad):
    part = lax.psum_scatter(
        grad.astype(jnp.bfloat16), "fsdp", scatter_dimension=0, tiled=True
    ).astype(jnp.float32)
    return lax.psum(part, "ctx")


def local(
    tokens,
    cotangent,
    lengths,
    block_table,
    qkv_weight,
    query_bias,
    value_bias,
    proj_weight,
    proj_bias,
    gain_first,
    shift_first,
    inner_weight,
    inner_bias,
    outer_weight,
    outer_bias,
    gain_second,
    shift_second,
):
    feat_width = HEADS * HEAD_DIM
    tok_rows = tokens.shape[0]
    seq_length = lengths[0]
    n_fsdp = lax.axis_size("fsdp")
    n_ctx = lax.axis_size("ctx")
    dealt = n_ctx == 8 and n_fsdp == 4 and tok_rows == 256
    vectors = (
        query_bias,
        value_bias,
        proj_bias,
        gain_first,
        shift_first,
        inner_bias,
        outer_bias,
        gain_second,
        shift_second,
    )
    ends = [0]
    for vector in vectors:
        ends.append(ends[-1] + vector.shape[0])
    gathered = lax.all_gather(jnp.concatenate(vectors)[None], "fsdp", axis=0, tiled=True)
    (
        qbias_full,
        vbias_full,
        pbias_full,
        gain1_full,
        shift1_full,
        ibias_full,
        obias_full,
        gain2_full,
        shift2_full,
    ) = [gathered[:, ends[k] : ends[k + 1]].reshape(-1) for k in range(len(vectors))]
    if dealt:
        both_full = gather_kernel_call(jnp.concatenate([qkv_weight, proj_weight], axis=1), 5)
        qkv_full = both_full[:, : 3 * feat_width]
        proj_full = both_full[:, 3 * feat_width :]
    else:
        qkv_full, proj_full, inner_full, outer_full = [
            lax.all_gather(weight, "fsdp", axis=0, tiled=True)
            for weight in (qkv_weight, proj_weight, inner_weight, outer_weight)
        ]
    tokens_wide = tokens.astype(jnp.float32)
    bias_row = jnp.concatenate([qbias_full, jnp.zeros_like(qbias_full), vbias_full]).astype(
        jnp.float32
    )
    packed = (jnp.dot(tokens, qkv_full, preferred_element_type=jnp.float32) + bias_row).astype(
        jnp.bfloat16
    )
    if dealt:
        context, saved, inner_full, outer_full = dealt_forward(
            packed, block_table, seq_length, n_ctx, inner_weight, outer_weight
        )
    else:
        context, saved = scan_forward(packed, block_table, seq_length)
    hidden = (
        tokens_wide
        + jnp.dot(context, proj_full, preferred_element_type=jnp.float32)
        + pbias_full.astype(jnp.float32)
    )
    normed, norm_back = jax.vjp(
        layer_norm, hidden, gain1_full.astype(jnp.float32), shift1_full.astype(jnp.float32)
    )
    normed_low = normed.astype(jnp.bfloat16)
    inner_pre = jnp.dot(
        normed_low, inner_full, preferred_element_type=jnp.float32
    ) + ibias_full.astype(jnp.float32)
    active, gelu_back = jax.vjp(gelu_exact, inner_pre)
    active_low = active.astype(jnp.bfloat16)
    mixed_sum = (
        normed
        + jnp.dot(active_low, outer_full, preferred_element_type=jnp.float32)
        + obias_full.astype(jnp.float32)
    )
    result, final_back = jax.vjp(
        layer_norm, mixed_sum, gain2_full.astype(jnp.float32), shift2_full.astype(jnp.float32)
    )
    layer_out = result.astype(jnp.bfloat16)
    mixed_grad, gain2_grad, shift2_grad = final_back(cotangent.astype(jnp.float32))
    branch_low = mixed_grad.astype(jnp.bfloat16)
    outer_grad = cross_dot(active_low, branch_low)
    obias_grad = jnp.sum(branch_low.astype(jnp.float32), axis=0)
    (inner_grad_wide,) = gelu_back(back_dot(branch_low, outer_full))
    inner_low = inner_grad_wide.astype(jnp.bfloat16)
    inner_grad = cross_dot(normed_low, inner_low)
    ibias_grad = jnp.sum(inner_low.astype(jnp.float32), axis=0)
    normed_grad = mixed_grad + back_dot(inner_low, inner_full)
    hidden_grad, gain1_grad, shift1_grad = norm_back(normed_grad)
    proj_low = hidden_grad.astype(jnp.bfloat16)
    proj_grad = cross_dot(context, proj_low)
    pbias_grad = jnp.sum(proj_low.astype(jnp.float32), axis=0)
    context_grad = back_dot(proj_low, proj_full).astype(jnp.bfloat16)
    if dealt:
        packed_grad = dealt_backward(context_grad, saved, n_ctx)
    else:
        packed_grad = scan_backward(context_grad, saved, block_table, seq_length)
    qkv_grad = cross_dot(tokens, packed_grad)
    qbias_grad = jnp.sum(packed_grad[:, :feat_width].astype(jnp.float32), axis=0)
    vbias_grad = jnp.sum(packed_grad[:, 2 * feat_width :].astype(jnp.float32), axis=0)
    tokens_grad = (hidden_grad + back_dot(packed_grad, qkv_full)).astype(jnp.bfloat16)
    sums = (
        qbias_grad,
        vbias_grad,
        pbias_grad,
        gain1_grad,
        shift1_grad,
        ibias_grad,
        obias_grad,
        gain2_grad,
        shift2_grad,
    )
    bundle = jnp.concatenate([total.reshape(n_fsdp, -1) for total in sums], axis=1)
    if dealt:
        bundle = reduce_bundle(bundle, n_ctx)
    else:
        bundle = lax.psum(bundle, ("fsdp", "ctx"))
        bundle = lax.dynamic_index_in_dim(bundle, lax.axis_index("fsdp"), axis=0, keepdims=False)
    vector_parts = [bundle[ends[k] : ends[k + 1]] for k in range(len(sums))]
    if dealt:
        low = jnp.bfloat16
        inner_sum, outer_sum, attn_sum = reduce_grads(
            [
                split_wide(inner_grad.astype(low)),
                outer_grad.astype(low).reshape(4, feat_width, feat_width),
                jnp.concatenate(
                    [
                        split_wide(qkv_grad.astype(low)),
                        proj_grad.astype(low).reshape(4, feat_width // 4, feat_width),
                    ],
                    axis=1,
                ),
            ]
        )
        shard_rows = feat_width // 4
        inner_sum = join_wide(inner_sum, shard_rows)
        qkv_sum = join_wide(attn_sum[: 3 * shard_rows], shard_rows)
        proj_sum = attn_sum[3 * shard_rows :]
    else:
        qkv_sum, proj_sum, inner_sum, outer_sum = [
            reduce_weight(grad) for grad in (qkv_grad, proj_grad, inner_grad, outer_grad)
        ]
    return (
        layer_out,
        tokens_grad,
        qkv_sum,
        vector_parts[0],
        vector_parts[1],
        proj_sum,
        vector_parts[2],
        vector_parts[3],
        vector_parts[4],
        inner_sum,
        vector_parts[5],
        outer_sum,
        vector_parts[6],
        vector_parts[7],
        vector_parts[8],
    )


def solution(mesh):
    placed = (
        P(("fsdp", "ctx"), None),
        P(("fsdp", "ctx"), None),
        P("fsdp"),
        P(),
        P("fsdp", None),
        P("fsdp"),
        P("fsdp"),
        P("fsdp", None),
        P("fsdp"),
        P("fsdp"),
        P("fsdp"),
        P("fsdp", None),
        P("fsdp"),
        P("fsdp", None),
        P("fsdp"),
        P("fsdp"),
        P("fsdp"),
    )
    return jax.shard_map(
        local,
        mesh=mesh,
        in_specs=placed,
        out_specs=(
            P(("fsdp", "ctx"), None),
            P(("fsdp", "ctx"), None),
            P("fsdp", None),
            P("fsdp"),
            P("fsdp"),
            P("fsdp", None),
            P("fsdp"),
            P("fsdp"),
            P("fsdp"),
            P("fsdp", None),
            P("fsdp"),
            P("fsdp", None),
            P("fsdp"),
            P("fsdp"),
            P("fsdp"),
        ),
        check_vma=False,
    )
```
